256 devices in a mesh: row: 16 (over z_lo, x), col: 16 (over y, z_hi, core).
Axes of the slice: x: 4, y: 4, z: 8 (z_hi: 2, z_lo: 4; z = z_hi * 4 + z_lo), core: 2. Of those that a mesh axis runs over, the one named last changes fastest.
Arguments:
- tiles: bfloat16 [1024, 64, 128, 128], P('row', 'col'), may hold values from -0.0625 to 0.0625
- pattern: int32 [1024, 64], P('row', 'col'), may hold values from 0 to 31, as said below
- omega: bfloat16 [65536, 128], P(('row', 'col')), may hold values from -6 to 6
Outputs:
- basis: float32 [65536, 128], P(('row', 'col'))
The draws below stay inside these ranges and needn't reach their ends.
Inputs may be any that keep to these rules, and one draw needn't show every extreme that they name: `pattern`: within each row block and index of col the 4 entries are distinct.
All inputs are finite; a program needn't handle non-finite values.
Results may differ from the reference program's by a relative error of at most 0.0065.
Values may be sent and summed in bfloat16 or wider, within the bound.
A program may use at most 128 MiB of HBM per device.

```python
import jax
import jax.numpy as jnp
from jax import lax

BS = 128
K = 128
TPC = 4
CG = 32
ROWBLOCKS = 1024
COLS = 65536
N_ROW = 16
N_COL = 16


def draw_pattern(key, part):
    key = jax.random.fold_in(key, 5)
    keys = jax.random.split(key, ROWBLOCKS * N_COL)
    picks = jax.vmap(lambda single: jax.random.permutation(single, CG)[:TPC])(keys)
    return picks.reshape(ROWBLOCKS, N_COL * TPC).astype(jnp.int32)


def block_scale(stream_key, extent, cuts, low, largest):
    gain, own = 1.0, jax.random.fold_in(stream_key, 6)
    for position, blocks in cuts:
        steps = jnp.exp(jax.random.uniform(jax.random.fold_in(own, position), (blocks,), jnp.float32, low / len(cuts), largest / len(cuts)))
        gain = gain * jnp.repeat(steps, extent[position] // blocks).reshape([-1 if axis == position else 1 for axis in range(len(extent))])
    return gain


def normal_values(rng, dims, spread, most, shards=(), kind=jnp.bfloat16):
    level = block_scale(rng, dims, shards, -0.22, 0.18) if shards else 1.0
    values = jax.random.normal(rng, dims, jnp.float32) * spread * level
    return jnp.minimum(jnp.maximum(values, -most), most).astype(kind)


def setup_inputs(seed: int = 0) -> dict:
    key_list = jax.random.split(jax.random.key(seed), 4)
    return {
        "tiles": normal_values(key_list[0], (ROWBLOCKS, N_COL * TPC, BS, BS), (TPC * N_COL * BS) ** -0.5, 0.0625, ((0, 16), (1, 16))),
        "pattern": draw_pattern(jax.random.fold_in(key_list[3], 71), 0),
        "omega": normal_values(key_list[2], (COLS, K), 1.0, 6.0, ((0, 256),)),
    }


def reference(tiles, pattern, omega):
    cpd = CG // N_ROW
    local = pattern.reshape(ROWBLOCKS, N_COL, TPC)
    colgroup = jnp.arange(N_COL, dtype=jnp.int32)[None, :, None]
    global_idx = (local // cpd * N_COL + colgroup) * cpd + local % cpd
    global_idx = global_idx.reshape(ROWBLOCKS, N_COL * TPC).astype(jnp.int32)
    blocks = omega.reshape(CG * N_COL, BS, K)

    def probe_row(args):
        tile_row, index_row = args
        chosen = blocks[index_row].astype(jnp.float32)
        return jnp.einsum('tab,tbk->ak', tile_row.astype(jnp.float32), chosen)
    probe = lax.map(probe_row, (tiles, global_idx)).astype(jnp.bfloat16)

    def accumulate(total, args):
        tile_row, index_row, probe_block = args
        terms = jnp.einsum('tab,ak->tbk', tile_row.astype(jnp.float32), probe_block.astype(jnp.float32))
        return (total.at[index_row].add(terms), None)
    sketch, unused = lax.scan(accumulate, jnp.zeros((CG * N_COL, BS, K), jnp.float32), (tiles, global_idx, probe))
    sketch = sketch.reshape(CG * N_COL * BS, K)
    gram = jnp.dot(sketch.T, sketch, precision=lax.Precision.HIGHEST)
    lower = jnp.linalg.cholesky(gram)
    solved = jax.scipy.linalg.solve_triangular(lower, sketch.T, lower=True)
    return solved.T * jnp.sqrt(jnp.float32(CG * N_COL * BS))
```

```python
import functools

import jax
import jax.numpy as jnp
from jax import lax
from jax.experimental import pallas as pl
from jax.experimental.pallas import tpu as pltpu
from jax.sharding import PartitionSpec as P

MESH = pl.DeviceIdType.MESH
BS = 128
F32 = jnp.float32
BF16 = jnp.bfloat16

OM_Z, OM_X, CORE_R, Y_R, Z_R, Y_G, CORE_G, SK_X, SK_Z, GR_P, GR_Z, GR_G = (
    0, 3, 15, 19, 31, 35, 47, 51, 63, 66, 98, 106)
N_SEM = 138


def outer_step(a, limit):
    rows = lax.broadcasted_iota(jnp.int32, (BS, BS), 0)
    cols = lax.broadcasted_iota(jnp.int32, (BS, BS), 1)
    done = []
    for k in range(8):
        row = a[k:k + 1, :]
        pivot = row[:, k:k + 1]
        col = jnp.broadcast_to(a[:, k:k + 1], (BS, BS))
        inv = 1.0 / pivot
        live = (rows > k) & (rows < limit)
        f = jnp.where(live, col * inv, 0.0)
        one = jnp.where(cols[:1] == k, 1.0, row)
        a = jnp.where(live & (cols == k), 0.0, a) - f * one
        done.append(pivot)
    return a, done


def lower_inverse(gram_ref, work_ref, piv_ref):
    work_ref[...] = gram_ref[...]

    def panel(p, carry):
        a, done = outer_step(work_ref[...], BS - 8 * p)
        piv_ref[pl.ds(pl.multiple_of(8 * p, 8), 8), :] = jnp.broadcast_to(
            jnp.concatenate(done, axis=0), (8, BS))
        a = jnp.concatenate([a[8:], a[:8]], axis=0)
        work_ref[...] = jnp.concatenate([a[:, 8:], a[:, :8]], axis=1)
        return carry

    lax.fori_loop(0, BS // 8, panel, 0)
    rows = lax.broadcasted_iota(jnp.int32, (BS, BS), 0)
    cols = lax.broadcasted_iota(jnp.int32, (BS, BS), 1)
    unit = jnp.where(rows > cols, work_ref[...], jnp.where(rows == cols, 1.0, 0.0))
    work_ref[...] = unit * lax.rsqrt(piv_ref[...])


def kernel(scale, pat, order, tiles_hbm, omega_hbm, out_ref,
           tiles, om, csend, crecv, own, ysend, yown, yrecv, zsend, zown, zrecv, probe_t, prefix, sk, skown,
           xrecv, zsum, zpiece, skrecv, skt, gpart, gown, grecv, gsum, gzrecv, gram, work, piv, ssem, rsem, lsem):
    r = lax.axis_index("row")
    c = lax.axis_index("col")
    zl, x = r // 4, r % 4
    y, zh, k = c // 4, (c // 2) % 2, c % 2

    def dev(zl=zl, x=x, y=y, zh=zh, k=k):
        return (zl * 4 + x, y * 4 + zh * 2 + k)

    def plane(d):
        n = ((x * 4 + y) * 2 + k + d) % 32
        return dev(x=n // 8, y=(n // 2) % 4, k=n % 2)

    def along_z(d):
        n = (zh * 4 + zl + d) % 8
        return dev(zh=n // 4, zl=n % 4)

    def send(src, dst, sem, where):
        pltpu.make_async_remote_copy(src_ref=src, dst_ref=dst, send_sem=ssem.at[sem], recv_sem=rsem.at[sem],
                                     device_id=where, device_id_type=MESH).start()

    def got(ref, sem):
        pltpu.make_async_copy(ref, ref, rsem.at[sem]).wait()

    def sent(ref, sem):
        pltpu.make_async_copy(ref, ref, ssem.at[sem]).wait()

    load_tiles = pltpu.make_async_copy(tiles_hbm, tiles, lsem.at[0])
    load_tiles.start()
    mine = om.at[pl.ds(2 * r, 2)]
    load_omega = pltpu.make_async_copy(omega_hbm, mine, lsem.at[1])
    load_omega.start()

    with jax.named_scope("barrier"):
        barrier = pltpu.get_barrier_semaphore()

        def greet_plane(d, carry):
            pl.semaphore_signal(barrier, inc=1, device_id=plane(d), device_id_type=MESH)
            return carry

        def greet_z(d, carry):
            pl.semaphore_signal(barrier, inc=1, device_id=along_z(d), device_id_type=MESH)
            return carry

        lax.fori_loop(1, 32, greet_plane, 0)
        lax.fori_loop(1, 8, greet_z, 0)
        load_omega.wait()
        pl.semaphore_wait(barrier, 38)

    with jax.named_scope("omega_gather"):
        for d in (3, 2, 1):
            send(mine, mine, OM_Z + d - 1, dev(zl=(zl + d) % 4))
        for dx in (1, 2, 3):
            send(mine, mine, OM_X + dx - 1, dev(x=(x + dx) % 4))
        for d in (1, 2, 3):
            block = om.at[pl.ds(2 * (((zl + 4 - d) % 4) * 4 + x), 2)]
            got(block, OM_Z + d - 1)
            for dx in (1, 2, 3):
                send(block, block, OM_X + d * 3 + dx - 1, dev(x=(x + dx) % 4))
        load_tiles.wait()
        for d in range(4):
            for dx in (1, 2, 3):
                got(om.at[pl.ds(2 * (((zl + 4 - d) % 4) * 4 + (x + 4 - dx) % 4), 2)], OM_X + d * 3 + dx - 1)
        for d in (1, 2, 3):
            sent(mine, OM_Z + d - 1)
        for d in range(4):
            for dx in (1, 2, 3):
                sent(mine, OM_X + d * 3 + dx - 1)

    def product(i):
        left = jnp.concatenate([tiles[i, t] for t in range(4)], axis=1)
        right = jnp.concatenate([om[pat[i, t]] for t in range(4)], axis=0)
        return jnp.dot(left, right, preferred_element_type=F32)

    def value_part(m):
        def for_sibling(b, carry):
            csend[m, b] = product(((1 - k) * 4 + m) * 8 + b).astype(BF16)
            return carry

        def for_own(b, carry):
            own[m, b] = product((k * 4 + m) * 8 + b)
            return carry

        lax.fori_loop(0, 8, for_sibling, 0, unroll=True)
        send(csend.at[m], crecv.at[m], CORE_R + m, dev(k=1 - k))
        lax.fori_loop(0, 8, for_own, 0, unroll=True)

    def along_y(m):
        got(crecv.at[m], CORE_R + m)
        for d in (1, 2, 3, 0):
            b = ((y + d) % 4) * 2
            total = own[m, pl.ds(b, 2)] + crecv[m, pl.ds(b, 2)].astype(F32)
            if d:
                ysend[m, d - 1] = total.astype(BF16)
                send(ysend.at[m, d - 1], yrecv.at[m, d - 1], Y_R + m * 3 + d - 1, dev(y=(y + d) % 4))
            else:
                yown[m] = total

    def across_z(m):
        total = yown[m]
        for d in (1, 2, 3):
            got(yrecv.at[m, d - 1], Y_R + m * 3 + d - 1)
            total += yrecv[m, d - 1].astype(F32)
        zown[m] = total
        zsend[m] = total.astype(BF16)
        send(zsend.at[m], zrecv.at[m], Z_R + m, dev(zh=1 - zh))

    def gather_y(m):
        got(zrecv.at[m], Z_R + m)
        total = zown[m] + zrecv[m].astype(F32)
        at = (k * 4 + m) * 8 + y * 2
        for b in range(2):
            probe_t[at + b] = total[b].T.astype(BF16)
        part = probe_t.at[pl.ds(at, 2)]
        for d in (1, 2, 3):
            send(part, part, Y_G + m * 3 + d - 1, dev(y=(y + d) % 4))

    def gather_core(m):
        for d in (1, 2, 3):
            got(probe_t.at[pl.ds((k * 4 + m) * 8 + ((y + 4 - d) % 4) * 2, 2)], Y_G + m * 3 + d - 1)
        part = probe_t.at[pl.ds((k * 4 + m) * 8, 8)]
        send(part, part, CORE_G + m, dev(k=1 - k))

    with jax.named_scope("probe_value"):
        value_part(0)
        value_part(1)
        along_y(0)
        value_part(2)
        along_y(1)
        value_part(3)
        along_y(2)
        along_y(3)
    with jax.named_scope("probe_sum"):
        across_z(0)
        across_z(1)
        across_z(2)
        gather_y(0)
        across_z(3)
        gather_y(1)
        gather_y(2)
        gather_core(0)
        gather_y(3)
        gather_core(1)
        gather_core(2)
        gather_core(3)
        for m in range(4):
            got(probe_t.at[pl.ds(((1 - k) * 4 + m) * 8, 8)], CORE_G + m)
        for m in range(4):
            sent(csend.at[m], CORE_R + m)
            sent(zsend.at[m], Z_R + m)
            sent(crecv.at[m], CORE_G + m)
            for d in range(3):
                sent(ysend.at[m, d], Y_R + m * 3 + d)
                sent(ysend.at[m, d], Y_G + m * 3 + d)

    with jax.named_scope("sketch_value"):
        def term(s, acc):
            e = order[s]
            keep = order[256 + s].astype(F32)
            acc = acc * keep + jnp.dot(probe_t[e // 4], tiles[e // 4, e % 4], preferred_element_type=F32)
            prefix[s] = acc
            return acc

        lax.fori_loop(0, 256, term, jnp.zeros((BS, BS), F32), unroll=8)

    with jax.named_scope("sketch_sum"):
        def column(p):
            return prefix[order[512 + p]] * order[544 + p].astype(F32)

        for dz in (1, 2, 3, 0):
            for dx in (1, 2, 3):
                to = ((zl + dz) % 4) * 4 + (x + dx) % 4
                for b in range(2):
                    sk[dz, dx - 1, b] = column(2 * to + b).astype(BF16)
                send(sk.at[dz, dx - 1], xrecv.at[dz, dx - 1], SK_X + dz * 3 + dx - 1, dev(x=(x + dx) % 4))
        for dz in (1, 2, 3, 0):
            for b in range(2):
                skown[dz, b] = column(2 * (((zl + dz) % 4) * 4 + x) + b)
        for dz in (1, 2, 3, 0):
            total = skown[dz]
            for dx in (1, 2, 3):
                got(xrecv.at[dz, dx - 1], SK_X + dz * 3 + dx - 1)
                total += xrecv[dz, dx - 1].astype(F32)
            if dz:
                zpiece[dz - 1] = total.astype(BF16)
                send(zpiece.at[dz - 1], skrecv.at[dz - 1], SK_Z + dz - 1, dev(zl=(zl + dz) % 4))
            else:
                zsum[...] = total
        total = zsum[...]
        for dz in (1, 2, 3):
            got(skrecv.at[dz - 1], SK_Z + dz - 1)
            total += skrecv[dz - 1].astype(F32)
        skt[:, :BS] = total[0]
        skt[:, BS:] = total[1]
        for dz in range(4):
            for dx in range(3):
                sent(sk.at[dz, dx], SK_X + dz * 3 + dx)
        for dz in range(3):
            sent(zpiece.at[dz], SK_Z + dz)

    with jax.named_scope("gram_sum"):
        g = lax.dot_general(skt[...], skt[...], (((1,), (1,)), ((), ())), precision=lax.Precision.HIGHEST,
                            preferred_element_type=F32)
        for n in range(32):
            gpart[n] = g[4 * n:4 * n + 4]
        here = (x * 4 + y) * 2 + k

        def spread(d, carry):
            send(gpart.at[(here + d) % 32], grecv.at[d - 1], GR_P + d, plane(d))
            return carry

        lax.fori_loop(1, 32, spread, 0)

        def collect(d, carry):
            got(grecv.at[d - 1], GR_P + d)
            return carry

        lax.fori_loop(1, 32, collect, 0)
        gsum[...] = gpart[here] + jnp.sum(grecv[...], axis=0)
        for d in range(1, 8):
            send(gsum, gzrecv.at[d - 1], GR_Z + d, along_z(d))
        for d in range(1, 8):
            got(gzrecv.at[d - 1], GR_Z + d)
        gown[here] = gsum[...] + jnp.sum(gzrecv[...], axis=0)

        def share(d, carry):
            send(gown.at[here], gown.at[here], GR_G + d, plane(d))
            return carry

        lax.fori_loop(1, 32, share, 0)

        def receive(d, carry):
            got(gown.at[(here + 32 - d) % 32], GR_G + d)
            return carry

        lax.fori_loop(1, 32, receive, 0)
        for n in range(32):
            gram[4 * n:4 * n + 4, :] = gown[n]

        def drain(d, carry):
            sent(gsum, GR_P + d)
            sent(gsum, GR_G + d)
            return carry

        lax.fori_loop(1, 32, drain, 0)
        for d in range(1, 8):
            sent(gsum, GR_Z + d)

    with jax.named_scope("cholesky"):
        lower_inverse(gram, work, piv)
    with jax.named_scope("basis"):
        basis_t = jnp.dot(work[...], skt[...], precision=lax.Precision.HIGHEST, preferred_element_type=F32)
        out_ref[...] = basis_t.T * scale


def sorted_order(pattern, groups):
    flat = pattern.reshape(-1)
    count = flat.shape[0]
    place = jnp.arange(count, dtype=jnp.int32)
    key = flat * count + place
    rank = jnp.sum((key[None, :] < key[:, None]).astype(jnp.int32), axis=1)
    at = rank[None, :] == place[:, None]
    tile = jnp.sum(jnp.where(at, place[None, :], 0), axis=1)
    block = jnp.sum(jnp.where(at, flat[None, :], 0), axis=1)
    keep = jnp.concatenate([jnp.zeros(1, jnp.int32), (block[1:] == block[:-1]).astype(jnp.int32)])
    wanted = jnp.arange(groups, dtype=jnp.int32)
    last = jnp.maximum(jnp.sum((flat[None, :] <= wanted[:, None]).astype(jnp.int32), axis=1) - 1, 0)
    some = jnp.any(flat[None, :] == wanted[:, None], axis=1).astype(jnp.int32)
    return jnp.concatenate([tile, keep, last, some])


def local(tiles, pattern, omega):
    scale = float(256 * omega.shape[0]) ** 0.5
    order = sorted_order(pattern, 32)
    vmem = pltpu.VMEM
    return pl.pallas_call(
        functools.partial(kernel, scale),
        name="gauss_newton_sketch",
        out_shape=jax.ShapeDtypeStruct((2 * BS, BS), F32),
        in_specs=[pl.BlockSpec(memory_space=pltpu.SMEM)] * 2 + [pl.BlockSpec(memory_space=pl.ANY)] * 2,
        out_specs=pl.BlockSpec(memory_space=vmem),
        scratch_shapes=[
            vmem((64, 4, BS, BS), BF16),
            vmem((32, BS, BS), BF16),
            vmem((4, 8, BS, BS), BF16),
            vmem((4, 8, BS, BS), BF16),
            vmem((4, 8, BS, BS), F32),
            vmem((4, 3, 2, BS, BS), BF16),
            vmem((4, 2, BS, BS), F32),
            vmem((4, 3, 2, BS, BS), BF16),
            vmem((4, 2, BS, BS), BF16),
            vmem((4, 2, BS, BS), F32),
            vmem((4, 2, BS, BS), BF16),
            vmem((64, BS, BS), BF16),
            vmem((256, BS, BS), F32),
            vmem((4, 3, 2, BS, BS), BF16),
            vmem((4, 2, BS, BS), F32),
            vmem((4, 3, 2, BS, BS), BF16),
            vmem((2, BS, BS), F32),
            vmem((3, 2, BS, BS), BF16),
            vmem((3, 2, BS, BS), BF16),
            vmem((BS, 2 * BS), F32),
            vmem((32, 4, BS), F32),
            vmem((32, 4, BS), F32),
            vmem((31, 4, BS), F32),
            vmem((4, BS), F32),
            vmem((7, 4, BS), F32),
            vmem((BS, BS), F32),
            vmem((BS, BS), F32),
            vmem((BS, BS), F32),
            pltpu.SemaphoreType.DMA((N_SEM,)),
            pltpu.SemaphoreType.DMA((N_SEM,)),
            pltpu.SemaphoreType.DMA((2,)),
        ],
        compiler_params=pltpu.CompilerParams(
            collective_id=0, has_side_effects=True, vmem_limit_bytes=56 * 1024 * 1024),
        cost_estimate=pl.CostEstimate(flops=2 * 2 * 256 * BS ** 3, bytes_accessed=9 * 2 ** 20, transcendentals=0),
    )(pattern, order, tiles, omega.reshape(2, BS, BS))


def solution(mesh):
    return jax.shard_map(
        local,
        mesh=mesh,
        in_specs=(P("row", "col", None, None), P("row", "col"), P(("row", "col"), None)),
        out_specs=P(("row", "col"), None),
        check_vma=False,
    )
```

```python
import functools

import jax
import jax.numpy as jnp
from jax import lax
from jax.experimental import pallas as pl
from jax.experimental.pallas import tpu as pltpu
from jax.sharding import PartitionSpec as P

MESH = pl.DeviceIdType.MESH
BS = 128
F32 = jnp.float32
BF16 = jnp.bfloat16

OM_Z, OM_X, CORE_R, Y_R, Z_R, Y_G, CORE_G, SK_X, SK_Z, GR_P, GR_Z, GR_G = (
    0, 3, 15, 19, 31, 35, 47, 51, 63, 66, 82, 98)
N_SEM = 114
PAIRS = 144


def over_lanes(v, k):
    return jnp.broadcast_to(v[:, k:k + 1], (8, BS))


def over_rows(v, k):
    return jnp.broadcast_to(v[k:k + 1, :], (8, BS))


def lower_inverse(gram, out):
    rows = lax.broadcasted_iota(jnp.int32, (8, BS), 0)
    cols = lax.broadcasted_iota(jnp.int32, (8, BS), 1)
    on = [cols == rows + 8 * p for p in range(16)]
    diag = [jnp.where(on[p], gram[p], 0.0) for p in range(16)]
    across = lax.rsqrt(jnp.sum(functools.reduce(jnp.add, diag), axis=0, keepdims=True))
    a = [gram[p] * lax.rsqrt(jnp.sum(diag[p], axis=1, keepdims=True)) * across for p in range(16)]
    for p in range(16):
        panel, first = a[p], 8 * p
        block = [over_lanes(panel, first + j) for j in range(8)]
        below = [[over_lanes(a[q], first + j) for j in range(8)] for q in range(p + 1, 16)]
        for j in range(0, 8, 2):
            k = first + j
            c0, c1 = block[j], block[j + 1]
            r0, r1 = over_rows(panel, j), over_rows(panel, j + 1)
            pa, pb, pc = over_rows(c0, j), over_rows(c0, j + 1), over_rows(c1, j + 1)
            det = pa * pc - pb * pb
            inv = 1.0 / det
            r0 = jnp.where(cols == k, 1.0, jnp.where(cols == k + 1, 0.0, r0))
            r1 = jnp.where(cols == k + 1, 1.0, jnp.where(cols == k, 0.0, r1))
            root = lax.rsqrt(pa)
            out[k:k + 1, :] = (jnp.where(cols <= k, r0, 0.0) * root * across)[0:1]
            low = r1 - (pb * (root * root)) * r0
            out[k + 1:k + 2, :] = (jnp.where(cols <= k + 1, low, 0.0) * (lax.rsqrt(det) * (pa * root)) * across)[0:1]
            f0 = jnp.where(rows == j, -1.0, jnp.where(rows == j + 1, 0.0, c0))
            f1 = jnp.where(rows == j + 1, -1.0, jnp.where(rows == j, 0.0, c1))
            g0, g1 = (f0 * pc - f1 * pb) * inv, (f1 * pa - f0 * pb) * inv
            pair = (rows == j) | (rows == j + 1)
            for i in range(j + 2, 8):
                block[i] = jnp.where(pair, 0.0, block[i]) - (
                    g0 * over_rows(block[i], j) + g1 * over_rows(block[i], j + 1))
            panel = jnp.where((cols == k) | (cols == k + 1) | pair, 0.0, panel) - (g0 * r0 + g1 * r1)
        inside = (cols >= first) & (cols < first + 8)
        r = [over_rows(panel, j) for j in range(8)]
        for q in range(p + 1, 16):
            b = below[q - p - 1]
            t = [b[j] * r[j] + b[j + 1] * r[j + 1] for j in range(0, 8, 2)]
            a[q] = jnp.where(inside, 0.0, a[q]) - ((t[0] + t[1]) + (t[2] + t[3]))


def sort_tiles(pat, meta):
    n, wanted = pat.shape[0], 3 * BS
    lane = lax.broadcasted_iota(jnp.int32, (n, BS), 1)
    pick = [pat[:, t:t + 1] for t in range(4)]
    hot = [jnp.where(jnp.broadcast_to(p, (n, BS)) == lane, 1, 0) for p in pick]
    total = (hot[0] + hot[1]) + (hot[2] + hot[3])
    upto = total
    for s in (1, 2, 4, 8, 16, 32):
        upto += jnp.concatenate([jnp.zeros((s, BS), jnp.int32), upto[:-s]], axis=0)
    before = upto - total
    count = upto[n - 1:]
    pairs = (count + 1) // 2
    ends = jnp.broadcast_to(pairs, (8, BS))
    for s in (1, 2, 4, 8, 16):
        ends += jnp.concatenate([jnp.zeros((8, s), jnp.int32), ends[:, :-s]], axis=1)
    base = ends[0:1] - pairs
    wide = lax.broadcasted_iota(jnp.int32, (n, wanted), 1)
    first = lax.broadcasted_iota(jnp.int32, (n, wanted), 0) * 4
    tile = jnp.zeros((1, wanted), jnp.int32)
    fresh = jnp.zeros((1, wanted), jnp.int32)
    flat = jnp.zeros((1, wanted), jnp.int32)
    for t in range(4):
        rank = jnp.sum(hot[t] * before, axis=1, keepdims=True)
        at = rank + 2 * jnp.sum(hot[t] * base, axis=1, keepdims=True)
        before = before + hot[t]
        tile += jnp.sum(jnp.where(at == wide, first + (t - 256), 0), axis=0, keepdims=True)
        fresh += jnp.sum(jnp.where((at == 2 * wide) & (rank == 0), 1, 0), axis=0, keepdims=True)
        flat += jnp.sum(jnp.where(first + t == wide, pick[t], 0), axis=0, keepdims=True)
    meta[...] = jnp.zeros_like(meta)
    meta[0:1, :] = jnp.clip(tile + 256, 0, 256)
    meta[1:2, :] = 1 - fresh
    meta[2:3, :BS] = jnp.clip(base + pairs - 1, 0, PAIRS - 1)
    meta[3:4, :BS] = jnp.minimum(count, 1)
    meta[4:5, :] = jnp.clip(flat, 0, 31)


def kernel(pat_hbm, tiles_hbm, omega_hbm, gown, skt,
           tiles, om, csend, crecv, own, ysend, yown, yrecv, zsend, zown, zrecv, probe_t, prefix, sk, skown,
           xrecv, zsum, zpiece, skrecv, gpart, grecv, gsum, gzrecv, pat, meta, order, ssem, rsem, lsem):
    r = lax.axis_index("row")
    c = lax.axis_index("col")
    zl, x = r // 4, r % 4
    y, zh, k = c // 4, (c // 2) % 2, c % 2

    def dev(zl=zl, x=x, y=y, zh=zh, k=k):
        return (zl * 4 + x, y * 4 + zh * 2 + k)

    xs = [(x + d) % 4 for d in range(4)]
    ys = [(y + d) % 4 for d in range(4)]
    zs = [(zh * 4 + zl + d) % 8 for d in range(8)]

    def plane(d):
        return dev(x=xs[d // 4], y=ys[d % 4])

    def column(d):
        return dev(zh=zs[d // 2] // 4, zl=zs[d // 2] % 4, k=(k + d) % 2)

    def send(src, dst, sem, where):
        pltpu.make_async_remote_copy(src_ref=src, dst_ref=dst, send_sem=ssem.at[sem], recv_sem=rsem.at[sem],
                                     device_id=where, device_id_type=MESH).start()

    def got(ref, sem):
        pltpu.make_async_copy(ref, ref, rsem.at[sem]).wait()

    def sent(ref, sem):
        pltpu.make_async_copy(ref, ref, ssem.at[sem]).wait()

    load_pattern = pltpu.make_async_copy(pat_hbm, pat, lsem.at[2])
    load_pattern.start()
    load_tiles = pltpu.make_async_copy(tiles_hbm, tiles.at[pl.ds(0, 64)], lsem.at[0])
    load_tiles.start()
    mine = om.at[pl.ds(2 * r, 2)]
    load_omega = pltpu.make_async_copy(omega_hbm, mine, lsem.at[1])
    load_omega.start()

    with jax.named_scope("barrier"):
        barrier = pltpu.get_barrier_semaphore()

        for d in range(1, 16):
            pl.semaphore_signal(barrier, inc=1, device_id=plane(d), device_id_type=MESH)
            pl.semaphore_signal(barrier, inc=1, device_id=column(d), device_id_type=MESH)
        load_omega.wait()
        pl.semaphore_wait(barrier, 30)

    load_order = pltpu.make_async_copy(meta, order, lsem.at[3])

    with jax.named_scope("omega_gather"):
        for d in (3, 2, 1):
            send(mine, mine, OM_Z + d - 1, dev(zl=(zl + d) % 4))
        for dx in (1, 2, 3):
            send(mine, mine, OM_X + dx - 1, dev(x=(x + dx) % 4))
        tiles[64, 0] = jnp.zeros((BS, BS), BF16)
        probe_t[64] = jnp.zeros((BS, BS), BF16)
        load_pattern.wait()
        sort_tiles(pat, meta)
        load_order.start()
        for d in (1, 2, 3):
            block = om.at[pl.ds(2 * (((zl + 4 - d) % 4) * 4 + x), 2)]
            got(block, OM_Z + d - 1)
            for dx in (1, 2, 3):
                send(block, block, OM_X + d * 3 + dx - 1, dev(x=(x + dx) % 4))
        load_tiles.wait()
        load_order.wait()
        for d in range(4):
            for dx in (1, 2, 3):
                got(om.at[pl.ds(2 * (((zl + 4 - d) % 4) * 4 + (x + 4 - dx) % 4), 2)], OM_X + d * 3 + dx - 1)
        for d in (1, 2, 3):
            sent(mine, OM_Z + d - 1)
        for d in range(4):
            for dx in (1, 2, 3):
                sent(mine, OM_X + d * 3 + dx - 1)

    def product(i):
        left = jnp.concatenate([tiles[i, t] for t in range(4)], axis=1)
        right = jnp.concatenate([om[order[4, 4 * i + t]] for t in range(4)], axis=0)
        return jnp.dot(left, right, preferred_element_type=F32)

    def value_part(m):
        def for_sibling(b, carry):
            csend[m, b] = product(((1 - k) * 4 + m) * 8 + b).astype(BF16)
            return carry

        def for_own(b, carry):
            own[m, b] = product((k * 4 + m) * 8 + b)
            return carry

        lax.fori_loop(0, 8, for_sibling, 0, unroll=True)
        send(csend.at[m], crecv.at[m], CORE_R + m, dev(k=1 - k))
        lax.fori_loop(0, 8, for_own, 0, unroll=True)

    def along_y(m):
        got(crecv.at[m], CORE_R + m)
        for d in (1, 2, 3, 0):
            b = ((y + d) % 4) * 2
            total = own[m, pl.ds(b, 2)] + crecv[m, pl.ds(b, 2)].astype(F32)
            if d:
                ysend[m, d - 1] = total.astype(BF16)
                send(ysend.at[m, d - 1], yrecv.at[m, d - 1], Y_R + m * 3 + d - 1, dev(y=(y + d) % 4))
            else:
                yown[m] = total

    def across_z(m):
        total = yown[m]
        for d in (1, 2, 3):
            got(yrecv.at[m, d - 1], Y_R + m * 3 + d - 1)
            total += yrecv[m, d - 1].astype(F32)
        zown[m] = total
        zsend[m] = total.astype(BF16)
        send(zsend.at[m], zrecv.at[m], Z_R + m, dev(zh=1 - zh))

    def gather_y(m):
        got(zrecv.at[m], Z_R + m)
        total = zown[m] + zrecv[m].astype(F32)
        at = (k * 4 + m) * 8 + y * 2
        for b in range(2):
            probe_t[at + b] = total[b].T.astype(BF16)
        part = probe_t.at[pl.ds(at, 2)]
        for d in (1, 2, 3):
            send(part, part, Y_G + m * 3 + d - 1, dev(y=(y + d) % 4))

    def gather_core(m):
        for d in (1, 2, 3):
            got(probe_t.at[pl.ds((k * 4 + m) * 8 + ((y + 4 - d) % 4) * 2, 2)], Y_G + m * 3 + d - 1)
        part = probe_t.at[pl.ds((k * 4 + m) * 8, 8)]
        send(part, part, CORE_G + m, dev(k=1 - k))

    with jax.named_scope("probe_sum"):
        value_part(0)
        along_y(0)
        value_part(1)
        along_y(1)
        value_part(2)
        along_y(2)
        across_z(0)
        value_part(3)
        along_y(3)
        across_z(1)
        across_z(2)
        gather_y(0)
        across_z(3)
        gather_y(1)
        gather_y(2)
        gather_core(0)
        gather_y(3)
        gather_core(1)
        gather_core(2)
        gather_core(3)
        for m in range(4):
            got(probe_t.at[pl.ds(((1 - k) * 4 + m) * 8, 8)], CORE_G + m)
        for m in range(4):
            sent(csend.at[m], CORE_R + m)
            sent(zsend.at[m], Z_R + m)
            sent(crecv.at[m], CORE_G + m)
            for d in range(3):
                sent(ysend.at[m, d], Y_R + m * 3 + d)
                sent(ysend.at[m, d], Y_G + m * 3 + d)

    with jax.named_scope("sketch_value"):
        def term(q, acc):
            e, f = order[0, 2 * q], order[0, 2 * q + 1]
            left = jnp.concatenate([probe_t[e // 4], probe_t[f // 4]], axis=1)
            right = jnp.concatenate([tiles[e // 4, e % 4], tiles[f // 4, f % 4]], axis=0)
            acc = acc * order[1, q].astype(F32) + jnp.dot(left, right, preferred_element_type=F32)
            prefix[q] = acc
            return acc

        lax.fori_loop(0, PAIRS, term, jnp.zeros((BS, BS), F32), unroll=8)

    with jax.named_scope("sketch_sum"):
        def block_sum(p):
            return prefix[order[2, p]] * order[3, p].astype(F32)

        for dz in (1, 2, 3, 0):
            for dx in (1, 2, 3):
                to = ((zl + dz) % 4) * 4 + (x + dx) % 4
                for b in range(2):
                    sk[dz, dx - 1, b] = block_sum(2 * to + b).astype(BF16)
                send(sk.at[dz, dx - 1], xrecv.at[dz, dx - 1], SK_X + dz * 3 + dx - 1, dev(x=(x + dx) % 4))
        for dz in (1, 2, 3, 0):
            for b in range(2):
                skown[dz, b] = block_sum(2 * (((zl + dz) % 4) * 4 + x) + b)
        for dz in (1, 2, 3, 0):
            total = skown[dz]
            for dx in (1, 2, 3):
                got(xrecv.at[dz, dx - 1], SK_X + dz * 3 + dx - 1)
                total += xrecv[dz, dx - 1].astype(F32)
            if dz:
                zpiece[dz - 1] = total.astype(BF16)
                send(zpiece.at[dz - 1], skrecv.at[dz - 1], SK_Z + dz - 1, dev(zl=(zl + dz) % 4))
            else:
                zsum[...] = total
        total = zsum[...]
        for dz in (1, 2, 3):
            got(skrecv.at[dz - 1], SK_Z + dz - 1)
            total += skrecv[dz - 1].astype(F32)
        skt[:, :BS] = total[0]
        skt[:, BS:] = total[1]
        for dz in range(4):
            for dx in range(3):
                sent(sk.at[dz, dx], SK_X + dz * 3 + dx)
        for dz in range(3):
            sent(zpiece.at[dz], SK_Z + dz)

    with jax.named_scope("gram_sum"):
        g = lax.dot_general(skt[...], skt[...], (((1,), (1,)), ((), ())), precision=lax.Precision.HIGHEST,
                            preferred_element_type=F32)
        gpart[...] = g.reshape(16, 8, BS)
        here = x * 4 + y

        def total(own, parts):
            parts = [own] + [parts[d] for d in range(15)]
            while len(parts) > 1:
                parts = [parts[i] + parts[i + 1] for i in range(0, len(parts), 2)]
            return parts[0]

        for d in range(1, 16):
            send(gpart.at[xs[d // 4] * 4 + ys[d % 4]], grecv.at[d - 1], GR_P + d, plane(d))
        for d in range(1, 16):
            got(grecv.at[d - 1], GR_P + d)
        gsum[...] = total(gpart[here], grecv)
        for d in range(1, 16):
            send(gsum, gzrecv.at[d - 1], GR_Z + d, column(d))
        for d in range(1, 16):
            got(gzrecv.at[d - 1], GR_Z + d)
        gown[here] = total(gsum[...], gzrecv)
        for d in range(1, 16):
            send(gown.at[here], gown.at[here], GR_G + d, plane(d))
        for d in range(1, 16):
            got(gown.at[xs[(4 - d // 4) % 4] * 4 + ys[(4 - d % 4) % 4]], GR_G + d)
        for d in range(1, 16):
            sent(gsum, GR_P + d)
            sent(gsum, GR_Z + d)
            sent(gsum, GR_G + d)


def finish(scale, gram, skt, out_ref, work):
    lower_inverse(gram, work)
    basis_t = jnp.dot(work[...], skt[...], precision=lax.Precision.HIGHEST, preferred_element_type=F32)
    out_ref[...] = basis_t.T * scale


def local(tiles, pattern, omega):
    scale = float(256 * omega.shape[0]) ** 0.5
    vmem = pltpu.VMEM
    gram, sketch_t = pl.pallas_call(
        kernel,
        name="gauss_newton_sketch",
        out_shape=[jax.ShapeDtypeStruct((16, 8, BS), F32), jax.ShapeDtypeStruct((BS, 2 * BS), F32)],
        in_specs=[pl.BlockSpec(memory_space=pl.ANY)] * 3,
        out_specs=[pl.BlockSpec(memory_space=vmem)] * 2,
        scratch_shapes=[
            vmem((65, 4, BS, BS), BF16),
            vmem((32, BS, BS), BF16),
            vmem((4, 8, BS, BS), BF16),
            vmem((4, 8, BS, BS), BF16),
            vmem((4, 8, BS, BS), F32),
            vmem((4, 3, 2, BS, BS), BF16),
            vmem((4, 2, BS, BS), F32),
            vmem((4, 3, 2, BS, BS), BF16),
            vmem((4, 2, BS, BS), BF16),
            vmem((4, 2, BS, BS), F32),
            vmem((4, 2, BS, BS), BF16),
            vmem((65, BS, BS), BF16),
            vmem((PAIRS, BS, BS), F32),
            vmem((4, 3, 2, BS, BS), BF16),
            vmem((4, 2, BS, BS), F32),
            vmem((4, 3, 2, BS, BS), BF16),
            vmem((2, BS, BS), F32),
            vmem((3, 2, BS, BS), BF16),
            vmem((3, 2, BS, BS), BF16),
            vmem((16, 8, BS), F32),
            vmem((15, 8, BS), F32),
            vmem((8, BS), F32),
            vmem((15, 8, BS), F32),
            vmem((64, 4), jnp.int32),
            vmem((8, 3 * BS), jnp.int32),
            pltpu.SMEM((8, 3 * BS), jnp.int32),
            pltpu.SemaphoreType.DMA((N_SEM,)),
            pltpu.SemaphoreType.DMA((N_SEM,)),
            pltpu.SemaphoreType.DMA((4,)),
        ],
        compiler_params=pltpu.CompilerParams(
            collective_id=0, has_side_effects=True, vmem_limit_bytes=56 * 1024 * 1024),
        cost_estimate=pl.CostEstimate(flops=2 * 2 * 256 * BS ** 3, bytes_accessed=9 * 2 ** 20, transcendentals=0),
    )(pattern, tiles, omega.reshape(2, BS, BS))
    return pl.pallas_call(
        functools.partial(finish, scale),
        name="cholesky_basis",
        out_shape=jax.ShapeDtypeStruct((2 * BS, BS), F32),
        in_specs=[pl.BlockSpec(memory_space=vmem)] * 2,
        out_specs=pl.BlockSpec(memory_space=vmem),
        scratch_shapes=[vmem((BS, BS), F32)],
    )(gram, sketch_t)


def solution(mesh):
    return jax.shard_map(
        local,
        mesh=mesh,
        in_specs=(P("row", "col", None, None), P("row", "col"), P(("row", "col"), None)),
        out_specs=P(("row", "col"), None),
        check_vma=False,
    )
```

```python
import functools

import jax
import jax.numpy as jnp
from jax import lax
from jax.experimental import pallas as pl
from jax.experimental.pallas import tpu as pltpu
from jax.sharding import PartitionSpec as P

MESH = pl.DeviceIdType.MESH
BS = 128
F32 = jnp.float32
BF16 = jnp.bfloat16

OM_Z, OM_X, CORE_R, Y_R, Z_R, Y_G, CORE_G, SK_X, SK_Z, GR_P, GR_Z, GR_G = (
    0, 3, 19, 23, 47, 51, 67, 71, 95, 98, 114, 130)
N_SEM = 146
PAIRS = 144


def over_lanes(v, k):
    return jnp.broadcast_to(v[:, k:k + 1], (8, BS))


def over_rows(v, k):
    return jnp.broadcast_to(v[k:k + 1, :], (8, BS))


def lower_inverse(gram, out):
    rows = lax.broadcasted_iota(jnp.int32, (8, BS), 0)
    cols = lax.broadcasted_iota(jnp.int32, (8, BS), 1)
    on = [cols == rows + 8 * p for p in range(16)]
    diag = [jnp.where(on[p], gram[p], 0.0) for p in range(16)]
    across = lax.rsqrt(jnp.sum(functools.reduce(jnp.add, diag), axis=0, keepdims=True))
    a = [gram[p] * lax.rsqrt(jnp.sum(diag[p], axis=1, keepdims=True)) * across for p in range(16)]
    for p in range(16):
        panel, first = a[p], 8 * p
        block = [over_lanes(panel, first + j) for j in range(8)]
        below = [[over_lanes(a[q], first + j) for j in range(8)] for q in range(p + 1, 16)]
        for j in range(0, 8, 2):
            k = first + j
            c0, c1 = block[j], block[j + 1]
            r0, r1 = over_rows(panel, j), over_rows(panel, j + 1)
            pa, pb, pc = over_rows(c0, j), over_rows(c0, j + 1), over_rows(c1, j + 1)
            det = pa * pc - pb * pb
            inv = 1.0 / det
            r0 = jnp.where(cols == k, 1.0, jnp.where(cols == k + 1, 0.0, r0))
            r1 = jnp.where(cols == k + 1, 1.0, jnp.where(cols == k, 0.0, r1))
            root = lax.rsqrt(pa)
            out[k:k + 1, :] = (jnp.where(cols <= k, r0, 0.0) * root * across)[0:1]
            low = r1 - (pb * (root * root)) * r0
            out[k + 1:k + 2, :] = (jnp.where(cols <= k + 1, low, 0.0) * (lax.rsqrt(det) * (pa * root)) * across)[0:1]
            f0 = jnp.where(rows == j, -1.0, jnp.where(rows == j + 1, 0.0, c0))
            f1 = jnp.where(rows == j + 1, -1.0, jnp.where(rows == j, 0.0, c1))
            g0, g1 = (f0 * pc - f1 * pb) * inv, (f1 * pa - f0 * pb) * inv
            pair = (rows == j) | (rows == j + 1)
            for i in range(j + 2, 8):
                block[i] = jnp.where(pair, 0.0, block[i]) - (
                    g0 * over_rows(block[i], j) + g1 * over_rows(block[i], j + 1))
            panel = jnp.where((cols == k) | (cols == k + 1) | pair, 0.0, panel) - (g0 * r0 + g1 * r1)
        inside = (cols >= first) & (cols < first + 8)
        r = [over_rows(panel, j) for j in range(8)]
        for q in range(p + 1, 16):
            b = below[q - p - 1]
            t = [b[j] * r[j] + b[j + 1] * r[j + 1] for j in range(0, 8, 2)]
            a[q] = jnp.where(inside, 0.0, a[q]) - ((t[0] + t[1]) + (t[2] + t[3]))


def sort_tiles(pat, meta):
    n, wanted = pat.shape[1], 3 * BS
    lane = lax.broadcasted_iota(jnp.int32, (n, BS), 1)
    wide_pat = jnp.concatenate([pat[...], jnp.zeros((4, BS - n), jnp.int32)], axis=1)
    tall = jnp.concatenate([wide_pat, jnp.zeros((4, BS), jnp.int32)], axis=0).T
    pick = [tall[:n, t:t + 1] for t in range(4)]
    hot = [jnp.where(jnp.broadcast_to(p, (n, BS)) == lane, 1, 0) for p in pick]
    total = (hot[0] + hot[1]) + (hot[2] + hot[3])
    upto = total
    for s in (1, 2, 4, 8, 16, 32):
        upto += jnp.concatenate([jnp.zeros((s, BS), jnp.int32), upto[:-s]], axis=0)
    before = upto - total
    count = upto[n - 1:]
    pairs = (count + 1) // 2
    ends = jnp.broadcast_to(pairs, (8, BS))
    for s in (1, 2, 4, 8, 16):
        ends += jnp.concatenate([jnp.zeros((8, s), jnp.int32), ends[:, :-s]], axis=1)
    base = ends[0:1] - pairs
    wide = lax.broadcasted_iota(jnp.int32, (n, wanted), 1)
    first = lax.broadcasted_iota(jnp.int32, (n, wanted), 0) * 4
    tile = jnp.zeros((1, wanted), jnp.int32)
    fresh = jnp.zeros((1, wanted), jnp.int32)
    flat = jnp.zeros((1, wanted), jnp.int32)
    for t in range(4):
        rank = jnp.sum(hot[t] * before, axis=1, keepdims=True)
        at = rank + 2 * jnp.sum(hot[t] * base, axis=1, keepdims=True)
        before = before + hot[t]
        tile += jnp.sum(jnp.where(at == wide, first + (t - 256), 0), axis=0, keepdims=True)
        fresh += jnp.sum(jnp.where((at == 2 * wide) & (rank == 0), 1, 0), axis=0, keepdims=True)
        flat += jnp.sum(jnp.where(first + t == wide, pick[t], 0), axis=0, keepdims=True)
    meta[...] = jnp.zeros_like(meta)
    meta[0:1, :] = jnp.clip(tile + 256, 0, 256)
    meta[1:2, :] = 1 - fresh
    meta[2:3, :BS] = jnp.clip(base + pairs - 1, 0, PAIRS - 1)
    meta[3:4, :BS] = jnp.minimum(count, 1)
    meta[4:5, :] = jnp.clip(flat, 0, 31)


def kernel(pat_hbm, tiles_hbm, omega_hbm, gown, skt,
           tiles, om, csend, crecv, own, ysend, yrecv, zsend, zown, zrecv, probe_t, prefix, sk,
           xrecv, zpiece, skrecv, gpart, grecv, gsum, gzrecv, pat, meta, order, ssem, rsem, lsem):
    r = lax.axis_index("row")
    c = lax.axis_index("col")
    zl, x = r // 4, r % 4
    y, zh, k = c // 4, (c // 2) % 2, c % 2

    def dev(zl=zl, x=x, y=y, zh=zh, k=k):
        return (zl * 4 + x, y * 4 + zh * 2 + k)

    xs = [(x + d) % 4 for d in range(4)]
    ys = [(y + d) % 4 for d in range(4)]
    zs = [(zh * 4 + zl + d) % 8 for d in range(8)]

    nearest = [jnp.where(zl == 0, a, jnp.where(zl == 3, b, e)) for a, b, e in ((3, 1, 1), (2, 2, 3), (1, 3, 2))]

    def plane(d):
        return dev(x=xs[d // 4], y=ys[d % 4])

    def column(d):
        return dev(zh=zs[d // 2] // 4, zl=zs[d // 2] % 4, k=(k + d) % 2)

    def send(src, dst, sem, where):
        pltpu.make_async_remote_copy(src_ref=src, dst_ref=dst, send_sem=ssem.at[sem], recv_sem=rsem.at[sem],
                                     device_id=where, device_id_type=MESH).start()

    def got(ref, sem):
        pltpu.make_async_copy(ref, ref, rsem.at[sem]).wait()

    def sent(ref, sem):
        pltpu.make_async_copy(ref, ref, ssem.at[sem]).wait()

    def drain(parts):
        for n in range(3):
            sent(zpiece.at[n], OM_Z + n)
            if parts == 3:
                sent(zpiece.at[n], SK_Z + n)
        for n in range(4):
            for j in range(3):
                sent(zsend.at[n], OM_X + n * 4 + j)
                if parts > 1:
                    sent(zsend.at[n], Y_G + n * 4 + j)
            if parts > 1:
                sent(csend.at[n], CORE_R + n)
                sent(csend.at[n], CORE_G + n)
                sent(zsend.at[n], Z_R + n)
            for j in range(6):
                if parts > 1 and j % 2 == 0:
                    sent(zsend.at[n], Y_R + n * 6 + j)
                if parts == 3:
                    sent(sk.at[n, j], SK_X + n * 6 + j)

    load_pattern = pltpu.make_async_copy(pat_hbm, pat, lsem.at[2])
    load_pattern.start()
    load_tiles = pltpu.make_async_copy(tiles_hbm, tiles.at[pl.ds(0, 64)], lsem.at[0])
    load_tiles.start()
    load_order = pltpu.make_async_copy(meta, order, lsem.at[3])
    mine = om.at[pl.ds(2 * r, 2)]
    load_omega = pltpu.make_async_copy(omega_hbm, mine, lsem.at[1])
    load_omega.start()

    with jax.named_scope("barrier"):
        barrier = pltpu.get_barrier_semaphore()

        for d in range(1, 16):
            pl.semaphore_signal(barrier, inc=1, device_id=plane(d), device_id_type=MESH)
            pl.semaphore_signal(barrier, inc=1, device_id=column(d), device_id_type=MESH)
        tiles[64, 0] = jnp.zeros((BS, BS), BF16)
        probe_t[64] = jnp.zeros((BS, BS), BF16)
        load_pattern.wait()
        sort_tiles(pat, meta)
        load_order.start()
        load_omega.wait()
        pl.semaphore_wait(barrier, 30)

    with jax.named_scope("omega_gather"):
        for d in nearest:
            send(mine, mine, OM_Z + 3 - d, dev(zl=(zl + 4 - d) % 4))

        def rows_of(back, dx):
            return 2 * (((zl + 4 - back) % 4) * 4 + xs[dx])

        def pass_on(n, back):
            block = om.at[pl.ds(rows_of(back, 0), 2)]
            if n:
                got(block, OM_Z + back - 1)
            send(block, block, OM_X + n * 4, dev(x=xs[1]))
            send(block, block, OM_X + n * 4 + 1, dev(x=xs[3]))
            send(block, block, OM_X + n * 4 + 2, dev(x=xs[2]))

        pass_on(0, 0)
        pass_on(1, nearest[0])
        pass_on(2, nearest[1])
        pass_on(3, nearest[2])
        load_tiles.wait()
        load_order.wait()
        for n, back in enumerate([0] + nearest):
            for j, dx in ((0, 3), (1, 1), (2, 2)):
                got(om.at[pl.ds(rows_of(back, dx), 2)], OM_X + n * 4 + j)

    def product(i):
        left = jnp.concatenate([tiles[i, t] for t in range(4)], axis=1)
        right = jnp.concatenate([om[order[4, 4 * i + t]] for t in range(4)], axis=0)
        return jnp.dot(left, right, preferred_element_type=F32)

    def value_part(m):
        def for_sibling(b, carry):
            csend[m, b] = product(((1 - k) * 4 + m) * 8 + b).astype(BF16)
            return carry

        def for_own(b, carry):
            own[m, b] = product((k * 4 + m) * 8 + b)
            return carry

        lax.fori_loop(0, 8, for_sibling, 0, unroll=True)
        send(csend.at[m], crecv.at[m], CORE_R + m, dev(k=1 - k))
        lax.fori_loop(0, 8, for_own, 0, unroll=True)

    def partial(m, dy, b):
        at = ys[dy] * 2 + b
        return own[m, at] + crecv[m, at].astype(F32)

    def along_y(m):
        got(crecv.at[m], CORE_R + m)
        for j, dy in ((0, 1), (2, 2), (4, 3)):
            for b in range(2):
                ysend[m, j + b] = partial(m, dy, b).astype(BF16)
            send(ysend.at[m, pl.ds(j, 2)], yrecv.at[m, pl.ds(j, 2)], Y_R + m * 6 + j, dev(y=ys[dy]))

    def across_z(m):
        for j in (0, 2, 4):
            got(yrecv.at[m, pl.ds(j, 2)], Y_R + m * 6 + j)
        for b in range(2):
            total = (partial(m, 0, b) + yrecv[m, b].astype(F32)) + (
                yrecv[m, 2 + b].astype(F32) + yrecv[m, 4 + b].astype(F32))
            zown[m, b] = total
            zsend[m, b] = total.astype(BF16)
        send(zsend.at[m], zrecv.at[m], Z_R + m, dev(zh=1 - zh))

    def gather_y(m):
        got(zrecv.at[m], Z_R + m)
        total = zown[m] + zrecv[m].astype(F32)
        at = (k * 4 + m) * 8 + y * 2
        for b in range(2):
            probe_t[at + b] = total[b].T.astype(BF16)
        part = probe_t.at[pl.ds(at, 2)]
        send(part, part, Y_G + m * 4, dev(y=ys[1]))
        send(part, part, Y_G + m * 4 + 1, dev(y=ys[3]))
        send(part, part, Y_G + m * 4 + 2, dev(y=ys[2]))

    def gather_core(m):
        for j, dy in ((0, 3), (1, 1), (2, 2)):
            got(probe_t.at[pl.ds((k * 4 + m) * 8 + ys[dy] * 2, 2)], Y_G + m * 4 + j)
        part = probe_t.at[pl.ds((k * 4 + m) * 8, 8)]
        send(part, part, CORE_G + m, dev(k=1 - k))

    with jax.named_scope("probe_sum"):
        for step, m in ((value_part, 0), (along_y, 0), (value_part, 1), (along_y, 1), (value_part, 2), (along_y, 2),
                        (across_z, 0), (value_part, 3), (along_y, 3), (across_z, 1), (across_z, 2), (gather_y, 0),
                        (across_z, 3), (gather_y, 1), (gather_y, 2), (gather_core, 0), (gather_y, 3), (gather_core, 1),
                        (gather_core, 2), (gather_core, 3)):
            step(m)
        for m in range(4):
            got(probe_t.at[pl.ds(((1 - k) * 4 + m) * 8, 8)], CORE_G + m)

    with jax.named_scope("sketch_value"):
        def term(q, acc):
            e, f = order[0, 2 * q], order[0, 2 * q + 1]
            left = jnp.concatenate([probe_t[e // 4], probe_t[f // 4]], axis=1)
            right = jnp.concatenate([tiles[e // 4, e % 4], tiles[f // 4, f % 4]], axis=0)
            acc = acc * order[1, q].astype(F32) + jnp.dot(left, right, preferred_element_type=F32)
            prefix[q] = acc
            return acc

        lax.fori_loop(0, PAIRS, term, jnp.zeros((BS, BS), F32), unroll=8)

    with jax.named_scope("sketch_sum"):
        def block_sum(p):
            return prefix[order[2, p]] * order[3, p].astype(F32)

        order_z = nearest[::-1] + [0]

        def term_of(n, dx, b):
            return block_sum(2 * (((zl + 4 - order_z[n]) % 4) * 4 + xs[dx]) + b)

        def send_x(n, j, value):
            sk[n, j] = value.astype(BF16)
            send(sk.at[n, j], xrecv.at[n, j], SK_X + n * 6 + j, dev(x=xs[1 if j % 2 == 0 else 3]))

        def got_x(n, j):
            got(xrecv.at[n, j], SK_X + n * 6 + j)
            return xrecv[n, j].astype(F32)

        def along_x(n):
            send_x(n, 0, term_of(n, 2, 0))
            send_x(n, 1, term_of(n, 2, 1))
            send_x(n, 2, term_of(n, 1, 1))
            send_x(n, 3, term_of(n, 3, 0))

        def relay_x(n):
            send_x(n, 4, term_of(n, 1, 0) + got_x(n, 0))
            send_x(n, 5, term_of(n, 3, 1) + got_x(n, 1))

        def across_zl(n):
            total = [term_of(n, 0, b) + got_x(n, i) + got_x(n, j) for b, (i, j) in enumerate(((3, 4), (2, 5)))]
            if n == 3:
                return total
            for b in range(2):
                zpiece[n, b] = total[b].astype(BF16)
            send(zpiece.at[n], skrecv.at[3 - order_z[n]], SK_Z + 3 - order_z[n], dev(zl=(zl + 4 - order_z[n]) % 4))

        for step, n in ((along_x, 0), (along_x, 1), (relay_x, 0), (along_x, 2), (relay_x, 1), (along_x, 3), (relay_x, 2),
                        (across_zl, 0), (relay_x, 3), (across_zl, 1), (across_zl, 2)):
            step(n)
        total = across_zl(3)
        for d in range(3):
            got(skrecv.at[d], SK_Z + d)
            for b in range(2):
                total[b] += skrecv[d, b].astype(F32)
        for b in range(2):
            skt[:, b * BS:(b + 1) * BS] = total[b]

    with jax.named_scope("gram_sum"):
        g = lax.dot_general(skt[...], skt[...], (((1,), (1,)), ((), ())), precision=lax.Precision.HIGHEST,
                            preferred_element_type=F32)
        gpart[...] = g.reshape(16, 8, BS)
        here = x * 4 + y

        def total(own, parts):
            parts = [own] + [parts[d] for d in range(15)]
            while len(parts) > 1:
                parts = [parts[i] + parts[i + 1] for i in range(0, len(parts), 2)]
            return parts[0]

        for d in range(1, 16):
            send(gpart.at[xs[d // 4] * 4 + ys[d % 4]], grecv.at[d - 1], GR_P + d, plane(d))
        for d in range(1, 16):
            got(grecv.at[d - 1], GR_P + d)
        gsum[...] = total(gpart[here], grecv)
        for d in range(1, 16):
            send(gsum, gzrecv.at[d - 1], GR_Z + d, column(d))
        for d in range(1, 16):
            got(gzrecv.at[d - 1], GR_Z + d)
        gown[here] = total(gsum[...], gzrecv)
        for d in range(1, 16):
            send(gown.at[here], gown.at[here], GR_G + d, plane(d))
        for d in range(1, 16):
            got(gown.at[xs[(4 - d // 4) % 4] * 4 + ys[(4 - d % 4) % 4]], GR_G + d)
        for d in range(1, 16):
            sent(gsum, GR_P + d)
            sent(gsum, GR_Z + d)
            sent(gsum, GR_G + d)
        drain(3)


def finish(scale, gram, skt, out_ref, work):
    lower_inverse(gram, work)
    basis_t = jnp.dot(work[...], skt[...], precision=lax.Precision.HIGHEST, preferred_element_type=F32)
    out_ref[...] = basis_t.T * scale


def local(tiles, pattern, omega):
    scale = float(256 * omega.shape[0]) ** 0.5
    vmem = pltpu.VMEM
    gram, sketch_t = pl.pallas_call(
        kernel,
        name="gauss_newton_sketch",
        out_shape=[jax.ShapeDtypeStruct((16, 8, BS), F32), jax.ShapeDtypeStruct((BS, 2 * BS), F32)],
        in_specs=[pl.BlockSpec(memory_space=pl.ANY)] * 3,
        out_specs=[pl.BlockSpec(memory_space=vmem)] * 2,
        scratch_shapes=[
            vmem((65, 4, BS, BS), BF16),
            vmem((32, BS, BS), BF16),
            vmem((4, 8, BS, BS), BF16),
            vmem((4, 8, BS, BS), BF16),
            vmem((4, 8, BS, BS), F32),
            vmem((4, 6, BS, BS), BF16),
            vmem((4, 6, BS, BS), BF16),
            vmem((4, 2, BS, BS), BF16),
            vmem((4, 2, BS, BS), F32),
            vmem((4, 2, BS, BS), BF16),
            vmem((65, BS, BS), BF16),
            vmem((PAIRS, BS, BS), F32),
            vmem((4, 6, BS, BS), BF16),
            vmem((4, 6, BS, BS), BF16),
            vmem((3, 2, BS, BS), BF16),
            vmem((3, 2, BS, BS), BF16),
            vmem((16, 8, BS), F32),
            vmem((15, 8, BS), F32),
            vmem((8, BS), F32),
            vmem((15, 8, BS), F32),
            vmem((4, 64), jnp.int32),
            vmem((8, 3 * BS), jnp.int32),
            pltpu.SMEM((8, 3 * BS), jnp.int32),
            pltpu.SemaphoreType.DMA((N_SEM,)),
            pltpu.SemaphoreType.DMA((N_SEM,)),
            pltpu.SemaphoreType.DMA((4,)),
        ],
        compiler_params=pltpu.CompilerParams(
            collective_id=0, has_side_effects=True, vmem_limit_bytes=56 * 1024 * 1024),
        cost_estimate=pl.CostEstimate(flops=2 * 2 * 256 * BS ** 3, bytes_accessed=9 * 2 ** 20, transcendentals=0),
    )(pattern.T, tiles, omega.reshape(2, BS, BS))
    return pl.pallas_call(
        functools.partial(finish, scale),
        name="cholesky_basis",
        out_shape=jax.ShapeDtypeStruct((2 * BS, BS), F32),
        in_specs=[pl.BlockSpec(memory_space=vmem)] * 2,
        out_specs=pl.BlockSpec(memory_space=vmem),
        scratch_shapes=[vmem((BS, BS), F32)],
    )(gram, sketch_t)


def solution(mesh):
    return jax.shard_map(
        local,
        mesh=mesh,
        in_specs=(P("row", "col", None, None), P("row", "col"), P(("row", "col"), None)),
        out_specs=P(("row", "col"), None),
        check_vma=False,
    )
```

```python
import functools

import jax
import jax.numpy as jnp
from jax import lax
from jax.experimental import pallas as pl
from jax.experimental.pallas import tpu as pltpu
from jax.sharding import PartitionSpec as P

MESH = pl.DeviceIdType.MESH
BS = 128
F32 = jnp.float32
BF16 = jnp.bfloat16

OM_Z, OM_X, CORE_R, Y_R, Z_R, Y_G, CORE_G, SK_X, SK_Z, GR_P, GR_Z, GR_G = (
    0, 3, 19, 23, 47, 55, 79, 83, 107, 110, 126, 142)
N_SEM = 158
PAIRS = 144


def over_lanes(v, k):
    return jnp.broadcast_to(v[:, k:k + 1], (8, BS))


def over_rows(v, k):
    return jnp.broadcast_to(v[k:k + 1, :], (8, BS))


def lower_inverse(gram, out):
    rows = lax.broadcasted_iota(jnp.int32, (8, BS), 0)
    cols = lax.broadcasted_iota(jnp.int32, (8, BS), 1)
    on = [cols == rows + 8 * p for p in range(16)]
    diag = [jnp.where(on[p], gram[p], 0.0) for p in range(16)]
    across = lax.rsqrt(jnp.sum(functools.reduce(jnp.add, diag), axis=0, keepdims=True))
    a = [gram[p] * lax.rsqrt(jnp.sum(diag[p], axis=1, keepdims=True)) * across for p in range(16)]
    for p in range(16):
        panel, first = a[p], 8 * p
        block = [over_lanes(panel, first + j) for j in range(8)]
        below = [[over_lanes(a[q], first + j) for j in range(8)] for q in range(p + 1, 16)]
        for j in range(0, 8, 2):
            k = first + j
            c0, c1 = block[j], block[j + 1]
            r0, r1 = over_rows(panel, j), over_rows(panel, j + 1)
            pa, pb, pc = over_rows(c0, j), over_rows(c0, j + 1), over_rows(c1, j + 1)
            det = pa * pc - pb * pb
            inv = 1.0 / det
            r0 = jnp.where(cols == k, 1.0, jnp.where(cols == k + 1, 0.0, r0))
            r1 = jnp.where(cols == k + 1, 1.0, jnp.where(cols == k, 0.0, r1))
            root = lax.rsqrt(pa)
            out[k:k + 1, :] = (jnp.where(cols <= k, r0, 0.0) * root * across)[0:1]
            low = r1 - (pb * (root * root)) * r0
            out[k + 1:k + 2, :] = (jnp.where(cols <= k + 1, low, 0.0) * (lax.rsqrt(det) * (pa * root)) * across)[0:1]
            f0 = jnp.where(rows == j, -1.0, jnp.where(rows == j + 1, 0.0, c0))
            f1 = jnp.where(rows == j + 1, -1.0, jnp.where(rows == j, 0.0, c1))
            g0, g1 = (f0 * pc - f1 * pb) * inv, (f1 * pa - f0 * pb) * inv
            pair = (rows == j) | (rows == j + 1)
            for i in range(j + 2, 8):
                block[i] = jnp.where(pair, 0.0, block[i]) - (
                    g0 * over_rows(block[i], j) + g1 * over_rows(block[i], j + 1))
            panel = jnp.where((cols == k) | (cols == k + 1) | pair, 0.0, panel) - (g0 * r0 + g1 * r1)
        inside = (cols >= first) & (cols < first + 8)
        r = [over_rows(panel, j) for j in range(8)]
        for q in range(p + 1, 16):
            b = below[q - p - 1]
            t = [b[j] * r[j] + b[j + 1] * r[j + 1] for j in range(0, 8, 2)]
            a[q] = jnp.where(inside, 0.0, a[q]) - ((t[0] + t[1]) + (t[2] + t[3]))


def sort_tiles(pat, meta):
    n, wanted = pat.shape[1], 3 * BS
    lane = lax.broadcasted_iota(jnp.int32, (n, BS), 1)
    wide_pat = jnp.concatenate([pat[...], jnp.zeros((4, BS - n), jnp.int32)], axis=1)
    tall = jnp.concatenate([wide_pat, jnp.zeros((4, BS), jnp.int32)], axis=0).T
    pick = [tall[:n, t:t + 1] for t in range(4)]
    hot = [jnp.where(jnp.broadcast_to(p, (n, BS)) == lane, 1, 0) for p in pick]
    total = (hot[0] + hot[1]) + (hot[2] + hot[3])
    upto = total
    for s in (1, 2, 4, 8, 16, 32):
        upto += jnp.concatenate([jnp.zeros((s, BS), jnp.int32), upto[:-s]], axis=0)
    before = upto - total
    count = upto[n - 1:]
    pairs = (count + 1) // 2
    ends = jnp.broadcast_to(pairs, (8, BS))
    for s in (1, 2, 4, 8, 16):
        ends += jnp.concatenate([jnp.zeros((8, s), jnp.int32), ends[:, :-s]], axis=1)
    base = ends[0:1] - pairs
    wide = lax.broadcasted_iota(jnp.int32, (n, wanted), 1)
    first = lax.broadcasted_iota(jnp.int32, (n, wanted), 0) * 4
    tile = jnp.zeros((1, wanted), jnp.int32)
    fresh = jnp.zeros((1, wanted), jnp.int32)
    flat = jnp.zeros((1, wanted), jnp.int32)
    for t in range(4):
        rank = jnp.sum(hot[t] * before, axis=1, keepdims=True)
        at = rank + 2 * jnp.sum(hot[t] * base, axis=1, keepdims=True)
        before = before + hot[t]
        tile += jnp.sum(jnp.where(at == wide, first + (t - 256), 0), axis=0, keepdims=True)
        fresh += jnp.sum(jnp.where((at == 2 * wide) & (rank == 0), 1, 0), axis=0, keepdims=True)
        flat += jnp.sum(jnp.where(first + t == wide, pick[t], 0), axis=0, keepdims=True)
    meta[...] = jnp.zeros_like(meta)
    meta[0:1, :] = jnp.clip(tile + 256, 0, 256)
    meta[1:2, :] = 1 - fresh
    meta[2:3, :BS] = jnp.clip(base + pairs - 1, 0, PAIRS - 1)
    meta[3:4, :BS] = jnp.minimum(count, 1)
    meta[4:5, :] = jnp.clip(flat, 0, 31)


def kernel(pat_hbm, tiles_hbm, omega_hbm, gown, skt,
           tiles, om, csend, crecv, own, ysend, yrecv, zsend, zown, zrecv, probe_t, prefix, sk,
           xrecv, zpiece, skrecv, gpart, grecv, gsum, gzrecv, pat, meta, order, ssem, rsem, lsem):
    r = lax.axis_index("row")
    c = lax.axis_index("col")
    zl, x = r // 4, r % 4
    y, zh, k = c // 4, (c // 2) % 2, c % 2

    def dev(zl=zl, x=x, y=y, zh=zh, k=k):
        return (zl * 4 + x, y * 4 + zh * 2 + k)

    xs = [(x + d) % 4 for d in range(4)]
    ys = [(y + d) % 4 for d in range(4)]
    zs = [(zh * 4 + zl + d) % 8 for d in range(8)]

    nearest = [jnp.where(zl == 0, a, jnp.where(zl == 3, b, e)) for a, b, e in ((3, 1, 1), (2, 2, 3), (1, 3, 2))]

    def plane(d):
        return dev(x=xs[d // 4], y=ys[d % 4])

    def column(d):
        return dev(zh=zs[d // 2] // 4, zl=zs[d // 2] % 4, k=(k + d) % 2)

    def send(src, dst, sem, where):
        pltpu.make_async_remote_copy(src_ref=src, dst_ref=dst, send_sem=ssem.at[sem], recv_sem=rsem.at[sem],
                                     device_id=where, device_id_type=MESH).start()

    def got(ref, sem):
        pltpu.make_async_copy(ref, ref, rsem.at[sem]).wait()

    def sent(ref, sem):
        pltpu.make_async_copy(ref, ref, ssem.at[sem]).wait()

    def drain(parts):
        for n in range(3):
            sent(zpiece.at[n], OM_Z + n)
            if parts == 3:
                sent(zpiece.at[n], SK_Z + n)
        for n in range(4):
            for j in range(3):
                sent(zsend.at[n], OM_X + n * 4 + j)
            if parts > 1:
                sent(csend.at[n], CORE_R + n)
                sent(csend.at[n], CORE_G + n)
                sent(zsend.at[n, 0], Z_R + n * 2)
                sent(zsend.at[n, 0], Z_R + n * 2 + 1)
            for j in range(6):
                if parts > 1:
                    sent(zsend.at[n, 0], Y_R + n * 6 + j)
                    sent(zsend.at[n, 0], Y_G + n * 6 + j)
                if parts == 3:
                    sent(sk.at[n, j], SK_X + n * 6 + j)

    load_pattern = pltpu.make_async_copy(pat_hbm, pat, lsem.at[2])
    load_pattern.start()
    load_tiles = pltpu.make_async_copy(tiles_hbm, tiles.at[pl.ds(0, 64)], lsem.at[0])
    load_tiles.start()
    load_order = pltpu.make_async_copy(meta, order, lsem.at[3])
    mine = om.at[pl.ds(2 * r, 2)]
    load_omega = pltpu.make_async_copy(omega_hbm, mine, lsem.at[1])
    load_omega.start()

    with jax.named_scope("barrier"):
        barrier = pltpu.get_barrier_semaphore()

        for d in range(1, 16):
            pl.semaphore_signal(barrier, inc=1, device_id=plane(d), device_id_type=MESH)
            pl.semaphore_signal(barrier, inc=1, device_id=column(d), device_id_type=MESH)
        tiles[64, 0] = jnp.zeros((BS, BS), BF16)
        probe_t[64] = jnp.zeros((BS, BS), BF16)
        load_pattern.wait()
        sort_tiles(pat, meta)
        load_order.start()
        load_omega.wait()
        pl.semaphore_wait(barrier, 30)

    with jax.named_scope("omega_gather"):
        for d in nearest:
            send(mine, mine, OM_Z + 3 - d, dev(zl=(zl + 4 - d) % 4))

        def rows_of(back, dx):
            return 2 * (((zl + 4 - back) % 4) * 4 + xs[dx])

        def pass_on(n, back):
            block = om.at[pl.ds(rows_of(back, 0), 2)]
            if n:
                got(block, OM_Z + back - 1)
            send(block, block, OM_X + n * 4, dev(x=xs[1]))
            send(block, block, OM_X + n * 4 + 1, dev(x=xs[3]))
            send(block, block, OM_X + n * 4 + 2, dev(x=xs[2]))

        pass_on(0, 0)
        pass_on(1, nearest[0])
        pass_on(2, nearest[1])
        pass_on(3, nearest[2])
        load_tiles.wait()
        load_order.wait()
        for n, back in enumerate([0] + nearest):
            for j, dx in ((0, 3), (1, 1), (2, 2)):
                got(om.at[pl.ds(rows_of(back, dx), 2)], OM_X + n * 4 + j)

    def product(i):
        left = jnp.concatenate([tiles[i, t] for t in range(4)], axis=1)
        right = jnp.concatenate([om[order[4, 4 * i + t]] for t in range(4)], axis=0)
        return jnp.dot(left, right, preferred_element_type=F32)

    def value_part(m):
        def for_sibling(b, carry):
            csend[m, b] = product(((1 - k) * 4 + m) * 8 + b).astype(BF16)
            return carry

        def for_own(b, carry):
            own[m, b] = product((k * 4 + m) * 8 + b)
            return carry

        lax.fori_loop(0, 8, for_sibling, 0, unroll=True)
        send(csend.at[m], crecv.at[m], CORE_R + m, dev(k=1 - k))
        lax.fori_loop(0, 8, for_own, 0, unroll=True)

    def partial(m, dy, b):
        at = ys[dy] * 2 + b
        return own[m, at] + crecv[m, at].astype(F32)

    def along_y(m):
        got(crecv.at[m], CORE_R + m)
        for b in range(2):
            for j, dy in ((2, 2), (0, 1), (4, 3)):
                ysend[m, j + b] = partial(m, dy, b).astype(BF16)
                send(ysend.at[m, j + b], yrecv.at[m, j + b], Y_R + m * 6 + j + b, dev(y=ys[dy]))

    def across_z(m, b):
        for j in (0, 2, 4):
            got(yrecv.at[m, j + b], Y_R + m * 6 + j + b)
        total = (partial(m, 0, b) + yrecv[m, b].astype(F32)) + (
            yrecv[m, 2 + b].astype(F32) + yrecv[m, 4 + b].astype(F32))
        zown[m, b] = total
        zsend[m, b] = total.astype(BF16)
        send(zsend.at[m, b], zrecv.at[m, b], Z_R + m * 2 + b, dev(zh=1 - zh))

    def gather_y(m, b):
        got(zrecv.at[m, b], Z_R + m * 2 + b)
        at = (k * 4 + m) * 8 + y * 2 + b
        probe_t[at] = (zown[m, b] + zrecv[m, b].astype(F32)).T.astype(BF16)
        part = probe_t.at[at]
        for j, dy in ((2, 2), (0, 1), (4, 3)):
            send(part, part, Y_G + m * 6 + j + b, dev(y=ys[dy]))

    def gather_core(m):
        for b in range(2):
            for j, dy in ((2, 2), (0, 3), (4, 1)):
                got(probe_t.at[(k * 4 + m) * 8 + ys[dy] * 2 + b], Y_G + m * 6 + j + b)
        part = probe_t.at[pl.ds((k * 4 + m) * 8, 8)]
        send(part, part, CORE_G + m, dev(k=1 - k))

    with jax.named_scope("probe_sum"):
        for step, *part in (
                (value_part, 0), (along_y, 0), (value_part, 1), (along_y, 1), (value_part, 2), (along_y, 2),
                (across_z, 0, 0), (across_z, 0, 1), (value_part, 3), (along_y, 3), (across_z, 1, 0), (across_z, 1, 1),
                (across_z, 2, 0), (gather_y, 0, 0), (across_z, 2, 1), (gather_y, 0, 1), (across_z, 3, 0),
                (gather_y, 1, 0), (across_z, 3, 1), (gather_y, 1, 1), (gather_y, 2, 0), (gather_core, 0),
                (gather_y, 2, 1), (gather_y, 3, 0), (gather_core, 1), (gather_y, 3, 1), (gather_core, 2),
                (gather_core, 3)):
            step(*part)
        for m in range(4):
            got(probe_t.at[pl.ds(((1 - k) * 4 + m) * 8, 8)], CORE_G + m)

    with jax.named_scope("sketch_value"):
        def term(q, acc):
            e, f = order[0, 2 * q], order[0, 2 * q + 1]
            left = jnp.concatenate([probe_t[e // 4], probe_t[f // 4]], axis=1)
            right = jnp.concatenate([tiles[e // 4, e % 4], tiles[f // 4, f % 4]], axis=0)
            acc = acc * order[1, q].astype(F32) + jnp.dot(left, right, preferred_element_type=F32)
            prefix[q] = acc
            return acc

        lax.fori_loop(0, PAIRS, term, jnp.zeros((BS, BS), F32), unroll=8)

    with jax.named_scope("sketch_sum"):
        def block_sum(p):
            return prefix[order[2, p]] * order[3, p].astype(F32)

        order_z = nearest[::-1] + [0]

        def term_of(n, dx, b):
            return block_sum(2 * (((zl + 4 - order_z[n]) % 4) * 4 + xs[dx]) + b)

        def send_x(n, j, value):
            sk[n, j] = value.astype(BF16)
            send(sk.at[n, j], xrecv.at[n, j], SK_X + n * 6 + j, dev(x=xs[1 if j % 2 == 0 else 3]))

        def got_x(n, j):
            got(xrecv.at[n, j], SK_X + n * 6 + j)
            return xrecv[n, j].astype(F32)

        def along_x(n):
            send_x(n, 0, term_of(n, 2, 0))
            send_x(n, 1, term_of(n, 2, 1))
            send_x(n, 2, term_of(n, 1, 1))
            send_x(n, 3, term_of(n, 3, 0))

        def relay_x(n):
            send_x(n, 4, term_of(n, 1, 0) + got_x(n, 0))
            send_x(n, 5, term_of(n, 3, 1) + got_x(n, 1))

        def across_zl(n):
            total = [term_of(n, 0, b) + got_x(n, i) + got_x(n, j) for b, (i, j) in enumerate(((3, 4), (2, 5)))]
            if n == 3:
                return total
            for b in range(2):
                zpiece[n, b] = total[b].astype(BF16)
            send(zpiece.at[n], skrecv.at[3 - order_z[n]], SK_Z + 3 - order_z[n], dev(zl=(zl + 4 - order_z[n]) % 4))

        for step, n in ((along_x, 0), (along_x, 1), (relay_x, 0), (along_x, 2), (relay_x, 1), (along_x, 3), (relay_x, 2),
                        (across_zl, 0), (relay_x, 3), (across_zl, 1), (across_zl, 2)):
            step(n)
        total = across_zl(3)
        for d in range(3):
            got(skrecv.at[d], SK_Z + d)
            for b in range(2):
                total[b] += skrecv[d, b].astype(F32)
        for b in range(2):
            skt[:, b * BS:(b + 1) * BS] = total[b]

    with jax.named_scope("gram_sum"):
        g = lax.dot_general(skt[...], skt[...], (((1,), (1,)), ((), ())), precision=lax.Precision.HIGHEST,
                            preferred_element_type=F32)
        gpart[...] = g.reshape(16, 8, BS)
        here = x * 4 + y

        def total(own, parts):
            parts = [own] + [parts[d] for d in range(15)]
            while len(parts) > 1:
                parts = [parts[i] + parts[i + 1] for i in range(0, len(parts), 2)]
            return parts[0]

        for d in range(1, 16):
            send(gpart.at[xs[d // 4] * 4 + ys[d % 4]], grecv.at[d - 1], GR_P + d, plane(d))
        for d in range(1, 16):
            got(grecv.at[d - 1], GR_P + d)
        gsum[...] = total(gpart[here], grecv)
        for d in range(1, 16):
            send(gsum, gzrecv.at[d - 1], GR_Z + d, column(d))
        for d in range(1, 16):
            got(gzrecv.at[d - 1], GR_Z + d)
        gown[here] = total(gsum[...], gzrecv)
        for d in range(1, 16):
            send(gown.at[here], gown.at[here], GR_G + d, plane(d))
        for d in range(1, 16):
            got(gown.at[xs[(4 - d // 4) % 4] * 4 + ys[(4 - d % 4) % 4]], GR_G + d)
        for d in range(1, 16):
            sent(gsum, GR_P + d)
            sent(gsum, GR_Z + d)
            sent(gsum, GR_G + d)
        drain(3)


def finish(scale, gram, skt, out_ref, work):
    lower_inverse(gram, work)
    basis_t = jnp.dot(work[...], skt[...], precision=lax.Precision.HIGHEST, preferred_element_type=F32)
    out_ref[...] = basis_t.T * scale


def local(tiles, pattern, omega):
    scale = float(256 * omega.shape[0]) ** 0.5
    vmem = pltpu.VMEM
    gram, sketch_t = pl.pallas_call(
        kernel,
        name="gauss_newton_sketch",
        out_shape=[jax.ShapeDtypeStruct((16, 8, BS), F32), jax.ShapeDtypeStruct((BS, 2 * BS), F32)],
        in_specs=[pl.BlockSpec(memory_space=pl.ANY)] * 3,
        out_specs=[pl.BlockSpec(memory_space=vmem)] * 2,
        scratch_shapes=[
            vmem((65, 4, BS, BS), BF16),
            vmem((32, BS, BS), BF16),
            vmem((4, 8, BS, BS), BF16),
            vmem((4, 8, BS, BS), BF16),
            vmem((4, 8, BS, BS), F32),
            vmem((4, 6, BS, BS), BF16),
            vmem((4, 6, BS, BS), BF16),
            vmem((4, 2, BS, BS), BF16),
            vmem((4, 2, BS, BS), F32),
            vmem((4, 2, BS, BS), BF16),
            vmem((65, BS, BS), BF16),
            vmem((PAIRS, BS, BS), F32),
            vmem((4, 6, BS, BS), BF16),
            vmem((4, 6, BS, BS), BF16),
            vmem((3, 2, BS, BS), BF16),
            vmem((3, 2, BS, BS), BF16),
            vmem((16, 8, BS), F32),
            vmem((15, 8, BS), F32),
            vmem((8, BS), F32),
            vmem((15, 8, BS), F32),
            vmem((4, 64), jnp.int32),
            vmem((8, 3 * BS), jnp.int32),
            pltpu.SMEM((8, 3 * BS), jnp.int32),
            pltpu.SemaphoreType.DMA((N_SEM,)),
            pltpu.SemaphoreType.DMA((N_SEM,)),
            pltpu.SemaphoreType.DMA((4,)),
        ],
        compiler_params=pltpu.CompilerParams(
            collective_id=0, has_side_effects=True, vmem_limit_bytes=56 * 1024 * 1024),
        cost_estimate=pl.CostEstimate(flops=2 * 2 * 256 * BS ** 3, bytes_accessed=9 * 2 ** 20, transcendentals=0),
    )(pattern.T, tiles, omega.reshape(2, BS, BS))
    return pl.pallas_call(
        functools.partial(finish, scale),
        name="cholesky_basis",
        out_shape=jax.ShapeDtypeStruct((2 * BS, BS), F32),
        in_specs=[pl.BlockSpec(memory_space=vmem)] * 2,
        out_specs=pl.BlockSpec(memory_space=vmem),
        scratch_shapes=[vmem((BS, BS), F32)],
    )(gram, sketch_t)


def solution(mesh):
    return jax.shard_map(
        local,
        mesh=mesh,
        in_specs=(P("row", "col", None, None), P("row", "col"), P(("row", "col"), None)),
        out_specs=P(("row", "col"), None),
        check_vma=False,
    )
```

```python
import functools

import jax
import jax.numpy as jnp
from jax import lax
from jax.experimental import pallas as pl
from jax.experimental.pallas import tpu as pltpu
from jax.sharding import PartitionSpec as P

MESH = pl.DeviceIdType.MESH
BS = 128
F32 = jnp.float32
BF16 = jnp.bfloat16

OM_Z, OM_X, CORE_R, Y_R, Z_R, Y_G, CORE_G, SK_X, SK_Z, GR_P, GR_Z, GR_G = (
    0, 6, 30, 34, 58, 66, 90, 94, 118, 124, 140, 156)
N_SEM = 172
PAIRS = 144


def over_lanes(v, k):
    return jnp.broadcast_to(v[:, k:k + 1], (8, BS))


def over_rows(v, k):
    return jnp.broadcast_to(v[k:k + 1, :], (8, BS))


def lower_inverse(gram, out):
    rows = lax.broadcasted_iota(jnp.int32, (8, BS), 0)
    cols = lax.broadcasted_iota(jnp.int32, (8, BS), 1)
    on = [cols == rows + 8 * p for p in range(16)]
    diag = [jnp.where(on[p], gram[p], 0.0) for p in range(16)]
    across = lax.rsqrt(jnp.sum(functools.reduce(jnp.add, diag), axis=0, keepdims=True))
    a = [gram[p] * lax.rsqrt(jnp.sum(diag[p], axis=1, keepdims=True)) * across for p in range(16)]
    for p in range(16):
        panel, first = a[p], 8 * p
        block = [over_lanes(panel, first + j) for j in range(8)]
        below = [[over_lanes(a[q], first + j) for j in range(8)] for q in range(p + 1, 16)]
        for j in range(0, 8, 2):
            k = first + j
            c0, c1 = block[j], block[j + 1]
            r0, r1 = over_rows(panel, j), over_rows(panel, j + 1)
            pa, pb, pc = over_rows(c0, j), over_rows(c0, j + 1), over_rows(c1, j + 1)
            det = pa * pc - pb * pb
            inv = 1.0 / det
            r0 = jnp.where(cols == k, 1.0, jnp.where(cols == k + 1, 0.0, r0))
            r1 = jnp.where(cols == k + 1, 1.0, jnp.where(cols == k, 0.0, r1))
            root = lax.rsqrt(pa)
            out[k:k + 1, :] = (jnp.where(cols <= k, r0, 0.0) * root * across)[0:1]
            low = r1 - (pb * (root * root)) * r0
            out[k + 1:k + 2, :] = (jnp.where(cols <= k + 1, low, 0.0) * (lax.rsqrt(det) * (pa * root)) * across)[0:1]
            f0 = jnp.where(rows == j, -1.0, jnp.where(rows == j + 1, 0.0, c0))
            f1 = jnp.where(rows == j + 1, -1.0, jnp.where(rows == j, 0.0, c1))
            g0, g1 = (f0 * pc - f1 * pb) * inv, (f1 * pa - f0 * pb) * inv
            pair = (rows == j) | (rows == j + 1)
            for i in range(j + 2, 8):
                block[i] = jnp.where(pair, 0.0, block[i]) - (
                    g0 * over_rows(block[i], j) + g1 * over_rows(block[i], j + 1))
            panel = jnp.where((cols == k) | (cols == k + 1) | pair, 0.0, panel) - (g0 * r0 + g1 * r1)
        inside = (cols >= first) & (cols < first + 8)
        r = [over_rows(panel, j) for j in range(8)]
        for q in range(p + 1, 16):
            b = below[q - p - 1]
            t = [b[j] * r[j] + b[j + 1] * r[j + 1] for j in range(0, 8, 2)]
            a[q] = jnp.where(inside, 0.0, a[q]) - ((t[0] + t[1]) + (t[2] + t[3]))


def sort_tiles(pat, meta):
    n, wanted = pat.shape[1], 3 * BS
    lane = lax.broadcasted_iota(jnp.int32, (n, BS), 1)
    wide_pat = jnp.concatenate([pat[...], jnp.zeros((4, BS - n), jnp.int32)], axis=1)
    tall = jnp.concatenate([wide_pat, jnp.zeros((4, BS), jnp.int32)], axis=0).T
    pick = [tall[:n, t:t + 1] for t in range(4)]
    hot = [jnp.where(jnp.broadcast_to(p, (n, BS)) == lane, 1, 0) for p in pick]
    total = (hot[0] + hot[1]) + (hot[2] + hot[3])
    upto = total
    for s in (1, 2, 4, 8, 16, 32):
        upto += jnp.concatenate([jnp.zeros((s, BS), jnp.int32), upto[:-s]], axis=0)
    before = upto - total
    count = upto[n - 1:]
    pairs = (count + 1) // 2
    ends = jnp.broadcast_to(pairs, (8, BS))
    for s in (1, 2, 4, 8, 16):
        ends += jnp.concatenate([jnp.zeros((8, s), jnp.int32), ends[:, :-s]], axis=1)
    base = ends[0:1] - pairs
    wide = lax.broadcasted_iota(jnp.int32, (n, wanted), 1)
    first = lax.broadcasted_iota(jnp.int32, (n, wanted), 0) * 4
    tile = jnp.zeros((1, wanted), jnp.int32)
    fresh = jnp.zeros((1, wanted), jnp.int32)
    flat = jnp.zeros((1, wanted), jnp.int32)
    for t in range(4):
        rank = jnp.sum(hot[t] * before, axis=1, keepdims=True)
        at = rank + 2 * jnp.sum(hot[t] * base, axis=1, keepdims=True)
        before = before + hot[t]
        tile += jnp.sum(jnp.where(at == wide, first + (t - 256), 0), axis=0, keepdims=True)
        fresh += jnp.sum(jnp.where((at == 2 * wide) & (rank == 0), 1, 0), axis=0, keepdims=True)
        flat += jnp.sum(jnp.where(first + t == wide, pick[t], 0), axis=0, keepdims=True)
    meta[...] = jnp.zeros_like(meta)
    meta[0:1, :] = jnp.clip(tile + 256, 0, 256)
    meta[1:2, :] = 1 - fresh
    meta[2:3, :BS] = jnp.clip(base + pairs - 1, 0, PAIRS - 1)
    meta[3:4, :BS] = jnp.minimum(count, 1)
    meta[4:5, :] = jnp.clip(flat, 0, 31)


def kernel(pat_hbm, tiles_hbm, omega_hbm, gown, skt,
           tiles, om, csend, crecv, own, ysend, yrecv, zsend, zown, zrecv, probe_t, prefix, sk,
           xrecv, zpiece, skrecv, gpart, grecv, gsum, gzrecv, pat, meta, order, ssem, rsem, lsem):
    r = lax.axis_index("row")
    c = lax.axis_index("col")
    zl, x = r // 4, r % 4
    y, zh, k = c // 4, (c // 2) % 2, c % 2

    def dev(zl=zl, x=x, y=y, zh=zh, k=k):
        return (zl * 4 + x, y * 4 + zh * 2 + k)

    xs = [(x + d) % 4 for d in range(4)]
    ys = [(y + d) % 4 for d in range(4)]
    zs = [(zh * 4 + zl + d) % 8 for d in range(8)]

    nearest = [jnp.where(zl == 0, a, jnp.where(zl == 3, b, e)) for a, b, e in ((3, 1, 1), (2, 2, 3), (1, 3, 2))]

    def plane(d):
        return dev(x=xs[d // 4], y=ys[d % 4])

    def column(d):
        return dev(zh=zs[d // 2] // 4, zl=zs[d // 2] % 4, k=(k + d) % 2)

    def send(src, dst, sem, where):
        pltpu.make_async_remote_copy(src_ref=src, dst_ref=dst, send_sem=ssem.at[sem], recv_sem=rsem.at[sem],
                                     device_id=where, device_id_type=MESH).start()

    def got(ref, sem):
        pltpu.make_async_copy(ref, ref, rsem.at[sem]).wait()

    def sent(ref, sem):
        pltpu.make_async_copy(ref, ref, ssem.at[sem]).wait()

    def drain(parts):
        for n in range(3):
            for b in range(2):
                sent(zpiece.at[n, b], OM_Z + n * 2 + b)
                if parts == 3:
                    sent(zpiece.at[n, b], SK_Z + n * 2 + b)
        for n in range(4):
            for j in range(6):
                sent(zsend.at[n, 0], OM_X + n * 6 + j)
            if parts > 1:
                sent(csend.at[n], CORE_R + n)
                sent(csend.at[n], CORE_G + n)
                sent(zsend.at[n, 0], Z_R + n * 2)
                sent(zsend.at[n, 0], Z_R + n * 2 + 1)
            for j in range(6):
                if parts > 1:
                    sent(zsend.at[n, 0], Y_R + n * 6 + j)
                    sent(zsend.at[n, 0], Y_G + n * 6 + j)
                if parts == 3:
                    sent(sk.at[n, j], SK_X + n * 6 + j)

    load_pattern = pltpu.make_async_copy(pat_hbm, pat, lsem.at[2])
    load_pattern.start()
    load_tiles = pltpu.make_async_copy(tiles_hbm, tiles.at[pl.ds(0, 64)], lsem.at[0])
    load_tiles.start()
    load_order = pltpu.make_async_copy(meta, order, lsem.at[3])
    mine = om.at[pl.ds(2 * r, 2)]
    load_omega = pltpu.make_async_copy(omega_hbm, mine, lsem.at[1])
    load_omega.start()

    with jax.named_scope("barrier"):
        barrier = pltpu.get_barrier_semaphore()

        for d in range(1, 16):
            pl.semaphore_signal(barrier, inc=1, device_id=plane(d), device_id_type=MESH)
            pl.semaphore_signal(barrier, inc=1, device_id=column(d), device_id_type=MESH)
        tiles[64, 0] = jnp.zeros((BS, BS), BF16)
        probe_t[64] = jnp.zeros((BS, BS), BF16)
        load_pattern.wait()
        sort_tiles(pat, meta)
        load_order.start()
        load_omega.wait()
        pl.semaphore_wait(barrier, 30)

    with jax.named_scope("omega_gather"):
        for d in nearest:
            for b in range(2):
                block = om.at[2 * r + b]
                send(block, block, OM_Z + (3 - d) * 2 + b, dev(zl=(zl + 4 - d) % 4))

        def rows_of(back, dx):
            return 2 * (((zl + 4 - back) % 4) * 4 + xs[dx])

        def pass_on(n, back):
            for b in range(2):
                block = om.at[rows_of(back, 0) + b]
                if n:
                    got(block, OM_Z + (back - 1) * 2 + b)
                for j, dx in ((2, 2), (0, 1), (4, 3)):
                    send(block, block, OM_X + n * 6 + j + b, dev(x=xs[dx]))

        pass_on(0, 0)
        pass_on(1, nearest[0])
        pass_on(2, nearest[1])
        pass_on(3, nearest[2])
        load_tiles.wait()
        load_order.wait()
        for n, back in enumerate([0] + nearest):
            for j, dx in ((0, 3), (4, 1), (2, 2)):
                for b in range(2):
                    got(om.at[rows_of(back, dx) + b], OM_X + n * 6 + j + b)

    def product(i):
        left = jnp.concatenate([tiles[i, t] for t in range(4)], axis=1)
        right = jnp.concatenate([om[order[4, 4 * i + t]] for t in range(4)], axis=0)
        return jnp.dot(left, right, preferred_element_type=F32)

    def value_part(m):
        def for_sibling(b, carry):
            csend[m, b] = product(((1 - k) * 4 + m) * 8 + b).astype(BF16)
            return carry

        def for_own(b, carry):
            own[m, b] = product((k * 4 + m) * 8 + b)
            return carry

        lax.fori_loop(0, 8, for_sibling, 0, unroll=True)
        send(csend.at[m], crecv.at[m], CORE_R + m, dev(k=1 - k))
        lax.fori_loop(0, 8, for_own, 0, unroll=True)

    def partial(m, dy, b):
        at = ys[dy] * 2 + b
        return own[m, at] + crecv[m, at].astype(F32)

    def along_y(m):
        got(crecv.at[m], CORE_R + m)
        for b in range(2):
            for j, dy in ((2, 2), (0, 1), (4, 3)):
                ysend[m, j + b] = partial(m, dy, b).astype(BF16)
                send(ysend.at[m, j + b], yrecv.at[m, j + b], Y_R + m * 6 + j + b, dev(y=ys[dy]))

    def across_z(m, b):
        for j in (0, 2, 4):
            got(yrecv.at[m, j + b], Y_R + m * 6 + j + b)
        total = (partial(m, 0, b) + yrecv[m, b].astype(F32)) + (
            yrecv[m, 2 + b].astype(F32) + yrecv[m, 4 + b].astype(F32))
        zown[m, b] = total
        zsend[m, b] = total.astype(BF16)
        send(zsend.at[m, b], zrecv.at[m, b], Z_R + m * 2 + b, dev(zh=1 - zh))

    def gather_y(m, b):
        got(zrecv.at[m, b], Z_R + m * 2 + b)
        at = (k * 4 + m) * 8 + y * 2 + b
        probe_t[at] = (zown[m, b] + zrecv[m, b].astype(F32)).T.astype(BF16)
        part = probe_t.at[at]
        for j, dy in ((2, 2), (0, 1), (4, 3)):
            send(part, part, Y_G + m * 6 + j + b, dev(y=ys[dy]))

    def gather_core(m):
        for b in range(2):
            for j, dy in ((2, 2), (0, 3), (4, 1)):
                got(probe_t.at[(k * 4 + m) * 8 + ys[dy] * 2 + b], Y_G + m * 6 + j + b)
        part = probe_t.at[pl.ds((k * 4 + m) * 8, 8)]
        send(part, part, CORE_G + m, dev(k=1 - k))

    with jax.named_scope("probe_sum"):
        for step, *part in (
                (value_part, 0), (along_y, 0), (value_part, 1), (along_y, 1), (value_part, 2), (along_y, 2),
                (across_z, 0, 0), (across_z, 0, 1), (value_part, 3), (along_y, 3), (across_z, 1, 0), (across_z, 1, 1),
                (across_z, 2, 0), (gather_y, 0, 0), (across_z, 2, 1), (gather_y, 0, 1), (across_z, 3, 0),
                (gather_y, 1, 0), (across_z, 3, 1), (gather_y, 1, 1), (gather_y, 2, 0), (gather_core, 0),
                (gather_y, 2, 1), (gather_y, 3, 0), (gather_core, 1), (gather_y, 3, 1), (gather_core, 2),
                (gather_core, 3)):
            step(*part)
        for m in range(4):
            got(probe_t.at[pl.ds(((1 - k) * 4 + m) * 8, 8)], CORE_G + m)

    with jax.named_scope("sketch_value"):
        def term(q, acc):
            e, f = order[0, 2 * q], order[0, 2 * q + 1]
            left = jnp.concatenate([probe_t[e // 4], probe_t[f // 4]], axis=1)
            right = jnp.concatenate([tiles[e // 4, e % 4], tiles[f // 4, f % 4]], axis=0)
            acc = acc * order[1, q].astype(F32) + jnp.dot(left, right, preferred_element_type=F32)
            prefix[q] = acc
            return acc

        lax.fori_loop(0, PAIRS, term, jnp.zeros((BS, BS), F32), unroll=8)

    with jax.named_scope("sketch_sum"):
        def block_sum(p):
            return prefix[order[2, p]] * order[3, p].astype(F32)

        order_z = nearest[::-1] + [0]

        def term_of(n, dx, b):
            return block_sum(2 * (((zl + 4 - order_z[n]) % 4) * 4 + xs[dx]) + b)

        def send_x(n, j, value):
            sk[n, j] = value.astype(BF16)
            send(sk.at[n, j], xrecv.at[n, j], SK_X + n * 6 + j, dev(x=xs[1 if j % 2 == 0 else 3]))

        def got_x(n, j):
            got(xrecv.at[n, j], SK_X + n * 6 + j)
            return xrecv[n, j].astype(F32)

        def along_x(n):
            send_x(n, 0, term_of(n, 2, 0))
            send_x(n, 1, term_of(n, 2, 1))
            send_x(n, 2, term_of(n, 1, 1))
            send_x(n, 3, term_of(n, 3, 0))

        def relay_x(n):
            send_x(n, 4, term_of(n, 1, 0) + got_x(n, 0))
            send_x(n, 5, term_of(n, 3, 1) + got_x(n, 1))

        def across_zl(n):
            total = []
            for b, (i, j) in enumerate(((3, 4), (2, 5))):
                total.append(term_of(n, 0, b) + got_x(n, i) + got_x(n, j))
                if n < 3:
                    zpiece[n, b] = total[b].astype(BF16)
                    to = 3 - order_z[n]
                    send(zpiece.at[n, b], skrecv.at[to, b], SK_Z + to * 2 + b, dev(zl=(zl + 4 - order_z[n]) % 4))
            return total

        for step, n in ((along_x, 0), (along_x, 1), (relay_x, 0), (along_x, 2), (relay_x, 1), (along_x, 3), (relay_x, 2),
                        (across_zl, 0), (relay_x, 3), (across_zl, 1), (across_zl, 2)):
            step(n)
        total = across_zl(3)
        for d in range(3):
            for b in range(2):
                got(skrecv.at[d, b], SK_Z + d * 2 + b)
                total[b] += skrecv[d, b].astype(F32)
        for b in range(2):
            skt[:, b * BS:(b + 1) * BS] = total[b]

    with jax.named_scope("gram_sum"):
        g = lax.dot_general(skt[...], skt[...], (((1,), (1,)), ((), ())), precision=lax.Precision.HIGHEST,
                            preferred_element_type=F32)
        gpart[...] = g.reshape(16, 8, BS)
        here = x * 4 + y

        def total(own, parts):
            parts = [own] + [parts[d] for d in range(15)]
            while len(parts) > 1:
                parts = [parts[i] + parts[i + 1] for i in range(0, len(parts), 2)]
            return parts[0]

        for d in range(1, 16):
            send(gpart.at[xs[d // 4] * 4 + ys[d % 4]], grecv.at[d - 1], GR_P + d, plane(d))
        for d in range(1, 16):
            got(grecv.at[d - 1], GR_P + d)
        gsum[...] = total(gpart[here], grecv)
        for d in range(1, 16):
            send(gsum, gzrecv.at[d - 1], GR_Z + d, column(d))
        for d in range(1, 16):
            got(gzrecv.at[d - 1], GR_Z + d)
        gown[here] = total(gsum[...], gzrecv)
        for d in range(1, 16):
            send(gown.at[here], gown.at[here], GR_G + d, plane(d))
        for d in range(1, 16):
            got(gown.at[xs[(4 - d // 4) % 4] * 4 + ys[(4 - d % 4) % 4]], GR_G + d)
        for d in range(1, 16):
            sent(gsum, GR_P + d)
            sent(gsum, GR_Z + d)
            sent(gsum, GR_G + d)
        drain(3)


def finish(scale, gram, skt, out_ref, work):
    lower_inverse(gram, work)
    basis_t = jnp.dot(work[...], skt[...], precision=lax.Precision.HIGHEST, preferred_element_type=F32)
    out_ref[...] = basis_t.T * scale


def local(tiles, pattern, omega):
    scale = float(256 * omega.shape[0]) ** 0.5
    vmem = pltpu.VMEM
    gram, sketch_t = pl.pallas_call(
        kernel,
        name="gauss_newton_sketch",
        out_shape=[jax.ShapeDtypeStruct((16, 8, BS), F32), jax.ShapeDtypeStruct((BS, 2 * BS), F32)],
        in_specs=[pl.BlockSpec(memory_space=pl.ANY)] * 3,
        out_specs=[pl.BlockSpec(memory_space=vmem)] * 2,
        scratch_shapes=[
            vmem((65, 4, BS, BS), BF16),
            vmem((32, BS, BS), BF16),
            vmem((4, 8, BS, BS), BF16),
            vmem((4, 8, BS, BS), BF16),
            vmem((4, 8, BS, BS), F32),
            vmem((4, 6, BS, BS), BF16),
            vmem((4, 6, BS, BS), BF16),
            vmem((4, 2, BS, BS), BF16),
            vmem((4, 2, BS, BS), F32),
            vmem((4, 2, BS, BS), BF16),
            vmem((65, BS, BS), BF16),
            vmem((PAIRS, BS, BS), F32),
            vmem((4, 6, BS, BS), BF16),
            vmem((4, 6, BS, BS), BF16),
            vmem((3, 2, BS, BS), BF16),
            vmem((3, 2, BS, BS), BF16),
            vmem((16, 8, BS), F32),
            vmem((15, 8, BS), F32),
            vmem((8, BS), F32),
            vmem((15, 8, BS), F32),
            vmem((4, 64), jnp.int32),
            vmem((8, 3 * BS), jnp.int32),
            pltpu.SMEM((8, 3 * BS), jnp.int32),
            pltpu.SemaphoreType.DMA((N_SEM,)),
            pltpu.SemaphoreType.DMA((N_SEM,)),
            pltpu.SemaphoreType.DMA((4,)),
        ],
        compiler_params=pltpu.CompilerParams(
            collective_id=0, has_side_effects=True, vmem_limit_bytes=56 * 1024 * 1024),
        cost_estimate=pl.CostEstimate(flops=2 * 2 * 256 * BS ** 3, bytes_accessed=9 * 2 ** 20, transcendentals=0),
    )(pattern.T, tiles, omega.reshape(2, BS, BS))
    return pl.pallas_call(
        functools.partial(finish, scale),
        name="cholesky_basis",
        out_shape=jax.ShapeDtypeStruct((2 * BS, BS), F32),
        in_specs=[pl.BlockSpec(memory_space=vmem)] * 2,
        out_specs=pl.BlockSpec(memory_space=vmem),
        scratch_shapes=[vmem((BS, BS), F32)],
    )(gram, sketch_t)


def solution(mesh):
    return jax.shard_map(
        local,
        mesh=mesh,
        in_specs=(P("row", "col", None, None), P("row", "col"), P(("row", "col"), None)),
        out_specs=P(("row", "col"), None),
        check_vma=False,
    )
```

```python
import functools

import jax
import jax.numpy as jnp
from jax import lax
from jax.experimental import pallas as pl
from jax.experimental.pallas import tpu as pltpu
from jax.sharding import PartitionSpec as P

MESH = pl.DeviceIdType.MESH
BS = 128
F32 = jnp.float32
BF16 = jnp.bfloat16

OM_Z, OM_X, CORE_R, Y_R, Z_R, Y_G, CORE_G, SK_X, SK_Z, GR_P, GR_Z, GR_G = (
    0, 6, 30, 34, 58, 66, 90, 94, 118, 124, 140, 156)
N_SEM = 172
PAIRS = 144


def over_lanes(v, k):
    return jnp.broadcast_to(v[:, k:k + 1], (8, BS))


def over_rows(v, k):
    return jnp.broadcast_to(v[k:k + 1, :], (8, BS))


def lower_inverse(gram, out):
    rows = lax.broadcasted_iota(jnp.int32, (8, BS), 0)
    cols = lax.broadcasted_iota(jnp.int32, (8, BS), 1)
    on = [cols == rows + 8 * p for p in range(16)]
    diag = [jnp.where(on[p], gram[p], 0.0) for p in range(16)]
    across = lax.rsqrt(jnp.sum(functools.reduce(jnp.add, diag), axis=0, keepdims=True))
    a = [gram[p] * lax.rsqrt(jnp.sum(diag[p], axis=1, keepdims=True)) * across for p in range(16)]
    for p in range(16):
        panel, first = a[p], 8 * p
        block = [over_lanes(panel, first + j) for j in range(8)]
        below = [[over_lanes(a[q], first + j) for j in range(8)] for q in range(p + 1, 16)]
        for j in range(0, 8, 2):
            k = first + j
            c0, c1 = block[j], block[j + 1]
            r0, r1 = over_rows(panel, j), over_rows(panel, j + 1)
            pa, pb, pc = over_rows(c0, j), over_rows(c0, j + 1), over_rows(c1, j + 1)
            det = pa * pc - pb * pb
            inv = 1.0 / det
            r0 = jnp.where(cols == k, 1.0, jnp.where(cols == k + 1, 0.0, r0))
            r1 = jnp.where(cols == k + 1, 1.0, jnp.where(cols == k, 0.0, r1))
            root = lax.rsqrt(pa)
            out[k:k + 1, :] = (jnp.where(cols <= k, r0, 0.0) * root * across)[0:1]
            low = r1 - (pb * (root * root)) * r0
            out[k + 1:k + 2, :] = (jnp.where(cols <= k + 1, low, 0.0) * (lax.rsqrt(det) * (pa * root)) * across)[0:1]
            f0 = jnp.where(rows == j, -1.0, jnp.where(rows == j + 1, 0.0, c0))
            f1 = jnp.where(rows == j + 1, -1.0, jnp.where(rows == j, 0.0, c1))
            g0, g1 = (f0 * pc - f1 * pb) * inv, (f1 * pa - f0 * pb) * inv
            pair = (rows == j) | (rows == j + 1)
            for i in range(j + 2, 8):
                block[i] = jnp.where(pair, 0.0, block[i]) - (
                    g0 * over_rows(block[i], j) + g1 * over_rows(block[i], j + 1))
            panel = jnp.where((cols == k) | (cols == k + 1) | pair, 0.0, panel) - (g0 * r0 + g1 * r1)
        inside = (cols >= first) & (cols < first + 8)
        r = [over_rows(panel, j) for j in range(8)]
        for q in range(p + 1, 16):
            b = below[q - p - 1]
            t = [b[j] * r[j] + b[j + 1] * r[j + 1] for j in range(0, 8, 2)]
            a[q] = jnp.where(inside, 0.0, a[q]) - ((t[0] + t[1]) + (t[2] + t[3]))


def sort_tiles(pat, meta):
    n, wanted = pat.shape[1], 3 * BS
    lane = lax.broadcasted_iota(jnp.int32, (n, BS), 1)
    wide_pat = jnp.concatenate([pat[...], jnp.zeros((4, BS - n), jnp.int32)], axis=1)
    tall = jnp.concatenate([wide_pat, jnp.zeros((4, BS), jnp.int32)], axis=0).T
    pick = [tall[:n, t:t + 1] for t in range(4)]
    hot = [jnp.where(jnp.broadcast_to(p, (n, BS)) == lane, 1, 0) for p in pick]
    total = (hot[0] + hot[1]) + (hot[2] + hot[3])
    upto = total
    for s in (1, 2, 4, 8, 16, 32):
        upto += jnp.concatenate([jnp.zeros((s, BS), jnp.int32), upto[:-s]], axis=0)
    before = upto - total
    count = upto[n - 1:]
    pairs = (count + 1) // 2
    ends = jnp.broadcast_to(pairs, (8, BS))
    for s in (1, 2, 4, 8, 16):
        ends += jnp.concatenate([jnp.zeros((8, s), jnp.int32), ends[:, :-s]], axis=1)
    base = ends[0:1] - pairs
    wide = lax.broadcasted_iota(jnp.int32, (n, wanted), 1)
    first = lax.broadcasted_iota(jnp.int32, (n, wanted), 0) * 4
    tile = jnp.zeros((1, wanted), jnp.int32)
    fresh = jnp.zeros((1, wanted), jnp.int32)
    flat = jnp.zeros((1, wanted), jnp.int32)
    for t in range(4):
        rank = jnp.sum(hot[t] * before, axis=1, keepdims=True)
        at = rank + 2 * jnp.sum(hot[t] * base, axis=1, keepdims=True)
        before = before + hot[t]
        tile += jnp.sum(jnp.where(at == wide, first + (t - 256), 0), axis=0, keepdims=True)
        fresh += jnp.sum(jnp.where((at == 2 * wide) & (rank == 0), 1, 0), axis=0, keepdims=True)
        flat += jnp.sum(jnp.where(first + t == wide, pick[t], 0), axis=0, keepdims=True)
    meta[...] = jnp.zeros_like(meta)
    meta[0:1, :] = jnp.clip(tile + 256, 0, 256)
    meta[1:2, :] = 1 - fresh
    meta[2:3, :BS] = jnp.clip(base + pairs - 1, 0, PAIRS - 1)
    meta[3:4, :BS] = jnp.minimum(count, 1)
    meta[4:5, :] = jnp.clip(flat, 0, 31)


def kernel(pat_hbm, tiles_hbm, omega_hbm, gown, skt,
           tiles, om, csend, crecv, own, ysend, yrecv, zsend, zown, zrecv, probe_t, prefix, sk,
           xrecv, zpiece, skrecv, gpart, grecv, gsum, gzrecv, pat, meta, order, ssem, rsem, lsem):
    r = lax.axis_index("row")
    c = lax.axis_index("col")
    zl, x = r // 4, r % 4
    y, zh, k = c // 4, (c // 2) % 2, c % 2

    def dev(zl=zl, x=x, y=y, zh=zh, k=k):
        return (zl * 4 + x, y * 4 + zh * 2 + k)

    xs = [(x + d) % 4 for d in range(4)]
    ys = [(y + d) % 4 for d in range(4)]
    zs = [(zh * 4 + zl + d) % 8 for d in range(8)]

    nearest = [jnp.where(zl == 0, a, jnp.where(zl == 3, b, e)) for a, b, e in ((3, 1, 1), (2, 2, 3), (1, 3, 2))]

    def plane(d):
        return dev(x=xs[d // 4], y=ys[d % 4])

    def column(d):
        return dev(zh=zs[d // 2] // 4, zl=zs[d // 2] % 4, k=(k + d) % 2)

    def send(src, dst, sem, where):
        pltpu.make_async_remote_copy(src_ref=src, dst_ref=dst, send_sem=ssem.at[sem], recv_sem=rsem.at[sem],
                                     device_id=where, device_id_type=MESH).start()

    def got(ref, sem):
        pltpu.make_async_copy(ref, ref, rsem.at[sem]).wait()

    def sent(ref, sem):
        pltpu.make_async_copy(ref, ref, ssem.at[sem]).wait()

    def drain(parts):
        for n in range(3):
            for b in range(2):
                sent(zpiece.at[n, b], OM_Z + n * 2 + b)
                if parts == 3:
                    sent(zpiece.at[n, b], SK_Z + n * 2 + b)
        for n in range(4):
            for j in range(6):
                sent(zsend.at[n, 0], OM_X + n * 6 + j)
            if parts > 1:
                sent(csend.at[n], CORE_R + n)
                sent(csend.at[n], CORE_G + n)
                sent(zsend.at[n, 0], Z_R + n * 2)
                sent(zsend.at[n, 0], Z_R + n * 2 + 1)
            for j in range(6):
                if parts > 1:
                    sent(zsend.at[n, 0], Y_R + n * 6 + j)
                    sent(zsend.at[n, 0], Y_G + n * 6 + j)
                if parts == 3:
                    sent(sk.at[n, j], SK_X + n * 6 + j)

    load_pattern = pltpu.make_async_copy(pat_hbm, pat, lsem.at[2])
    load_pattern.start()
    load_tiles = pltpu.make_async_copy(tiles_hbm, tiles.at[pl.ds(0, 64)], lsem.at[0])
    load_order = pltpu.make_async_copy(meta, order, lsem.at[3])
    mine = om.at[pl.ds(2 * r, 2)]
    load_omega = pltpu.make_async_copy(omega_hbm, mine, lsem.at[1])
    load_omega.start()
    load_tiles.start()

    with jax.named_scope("barrier"):
        barrier = pltpu.get_barrier_semaphore()

        for d in range(1, 16):
            pl.semaphore_signal(barrier, inc=1, device_id=plane(d), device_id_type=MESH)
            pl.semaphore_signal(barrier, inc=1, device_id=column(d), device_id_type=MESH)
        load_omega.wait()
        pl.semaphore_wait(barrier, 30)

    with jax.named_scope("omega_gather"):
        for d in nearest:
            for b in range(2):
                block = om.at[2 * r + b]
                send(block, block, OM_Z + (3 - d) * 2 + b, dev(zl=(zl + 4 - d) % 4))

        def rows_of(back, dx):
            return 2 * (((zl + 4 - back) % 4) * 4 + xs[dx])

        def pass_on(n, back):
            for b in range(2):
                block = om.at[rows_of(back, 0) + b]
                if n:
                    got(block, OM_Z + (back - 1) * 2 + b)
                for j, dx in ((2, 2), (0, 1), (4, 3)):
                    send(block, block, OM_X + n * 6 + j + b, dev(x=xs[dx]))

        pass_on(0, 0)
        tiles[64, 0] = jnp.zeros((BS, BS), BF16)
        probe_t[64] = jnp.zeros((BS, BS), BF16)
        load_pattern.wait()
        sort_tiles(pat, meta)
        load_order.start()
        pass_on(1, nearest[0])
        pass_on(2, nearest[1])
        pass_on(3, nearest[2])
        load_tiles.wait()
        load_order.wait()
        for n, back in enumerate([0] + nearest):
            for j, dx in ((0, 3), (4, 1), (2, 2)):
                for b in range(2):
                    got(om.at[rows_of(back, dx) + b], OM_X + n * 6 + j + b)

    def product(i):
        left = jnp.concatenate([tiles[i, t] for t in range(4)], axis=1)
        right = jnp.concatenate([om[order[4, 4 * i + t]] for t in range(4)], axis=0)
        return jnp.dot(left, right, preferred_element_type=F32)

    def value_part(m):
        def for_sibling(b, carry):
            csend[m, b] = product(((1 - k) * 4 + m) * 8 + b).astype(BF16)
            return carry

        def for_own(b, carry):
            own[m, b] = product((k * 4 + m) * 8 + b)
            return carry

        lax.fori_loop(0, 8, for_sibling, 0, unroll=True)
        send(csend.at[m], crecv.at[m], CORE_R + m, dev(k=1 - k))
        lax.fori_loop(0, 8, for_own, 0, unroll=True)

    def partial(m, dy, b):
        at = ys[dy] * 2 + b
        return own[m, at] + crecv[m, at].astype(F32)

    def along_y(m):
        got(crecv.at[m], CORE_R + m)
        for b in range(2):
            for j, dy in ((2, 2), (0, 1), (4, 3)):
                ysend[m, j + b] = partial(m, dy, b).astype(BF16)
                send(ysend.at[m, j + b], yrecv.at[m, j + b], Y_R + m * 6 + j + b, dev(y=ys[dy]))

    def across_z(m, b):
        for j in (0, 2, 4):
            got(yrecv.at[m, j + b], Y_R + m * 6 + j + b)
        total = (partial(m, 0, b) + yrecv[m, b].astype(F32)) + (
            yrecv[m, 2 + b].astype(F32) + yrecv[m, 4 + b].astype(F32))
        zown[m, b] = total
        zsend[m, b] = total.astype(BF16)
        send(zsend.at[m, b], zrecv.at[m, b], Z_R + m * 2 + b, dev(zh=1 - zh))

    def gather_y(m, b):
        got(zrecv.at[m, b], Z_R + m * 2 + b)
        at = (k * 4 + m) * 8 + y * 2 + b
        probe_t[at] = (zown[m, b] + zrecv[m, b].astype(F32)).T.astype(BF16)
        part = probe_t.at[at]
        for j, dy in ((2, 2), (0, 1), (4, 3)):
            send(part, part, Y_G + m * 6 + j + b, dev(y=ys[dy]))

    def gather_core(m):
        for b in range(2):
            for j, dy in ((2, 2), (0, 3), (4, 1)):
                got(probe_t.at[(k * 4 + m) * 8 + ys[dy] * 2 + b], Y_G + m * 6 + j + b)
        part = probe_t.at[pl.ds((k * 4 + m) * 8, 8)]
        send(part, part, CORE_G + m, dev(k=1 - k))

    with jax.named_scope("probe_sum"):
        for step, *part in (
                (value_part, 0), (along_y, 0), (value_part, 1), (along_y, 1), (value_part, 2), (along_y, 2),
                (across_z, 0, 0), (across_z, 0, 1), (value_part, 3), (along_y, 3), (across_z, 1, 0), (across_z, 1, 1),
                (across_z, 2, 0), (gather_y, 0, 0), (across_z, 2, 1), (gather_y, 0, 1), (across_z, 3, 0),
                (gather_y, 1, 0), (across_z, 3, 1), (gather_y, 1, 1), (gather_y, 2, 0), (gather_core, 0),
                (gather_y, 2, 1), (gather_y, 3, 0), (gather_core, 1), (gather_y, 3, 1), (gather_core, 2),
                (gather_core, 3)):
            step(*part)
        for m in range(4):
            got(probe_t.at[pl.ds(((1 - k) * 4 + m) * 8, 8)], CORE_G + m)

    with jax.named_scope("sketch_value"):
        def term(q, acc):
            e, f = order[0, 2 * q], order[0, 2 * q + 1]
            left = jnp.concatenate([probe_t[e // 4], probe_t[f // 4]], axis=1)
            right = jnp.concatenate([tiles[e // 4, e % 4], tiles[f // 4, f % 4]], axis=0)
            acc = acc * order[1, q].astype(F32) + jnp.dot(left, right, preferred_element_type=F32)
            prefix[q] = acc
            return acc

        lax.fori_loop(0, PAIRS, term, jnp.zeros((BS, BS), F32), unroll=8)

    with jax.named_scope("sketch_sum"):
        def block_sum(p):
            return prefix[order[2, p]] * order[3, p].astype(F32)

        order_z = nearest[::-1] + [0]

        def term_of(n, dx, b):
            return block_sum(2 * (((zl + 4 - order_z[n]) % 4) * 4 + xs[dx]) + b)

        def send_x(n, j, value):
            sk[n, j] = value.astype(BF16)
            send(sk.at[n, j], xrecv.at[n, j], SK_X + n * 6 + j, dev(x=xs[1 if j % 2 == 0 else 3]))

        def got_x(n, j):
            got(xrecv.at[n, j], SK_X + n * 6 + j)
            return xrecv[n, j].astype(F32)

        def along_x(n):
            send_x(n, 0, term_of(n, 2, 0))
            send_x(n, 1, term_of(n, 2, 1))
            send_x(n, 2, term_of(n, 1, 1))
            send_x(n, 3, term_of(n, 3, 0))

        def relay_x(n):
            send_x(n, 4, term_of(n, 1, 0) + got_x(n, 0))
            send_x(n, 5, term_of(n, 3, 1) + got_x(n, 1))

        def across_zl(n):
            total = []
            for b, (i, j) in enumerate(((3, 4), (2, 5))):
                total.append(term_of(n, 0, b) + got_x(n, i) + got_x(n, j))
                if n < 3:
                    zpiece[n, b] = total[b].astype(BF16)
                    to = 3 - order_z[n]
                    send(zpiece.at[n, b], skrecv.at[to, b], SK_Z + to * 2 + b, dev(zl=(zl + 4 - order_z[n]) % 4))
            return total

        for step, n in ((along_x, 0), (along_x, 1), (relay_x, 0), (along_x, 2), (relay_x, 1), (along_x, 3), (relay_x, 2),
                        (across_zl, 0), (relay_x, 3), (across_zl, 1), (across_zl, 2)):
            step(n)
        total = across_zl(3)
        for d in range(3):
            for b in range(2):
                got(skrecv.at[d, b], SK_Z + d * 2 + b)
                total[b] += skrecv[d, b].astype(F32)
        for b in range(2):
            skt[:, b * BS:(b + 1) * BS] = total[b]

    with jax.named_scope("gram_sum"):
        g = lax.dot_general(skt[...], skt[...], (((1,), (1,)), ((), ())), precision=lax.Precision.HIGHEST,
                            preferred_element_type=F32)
        gpart[...] = g.reshape(16, 8, BS)
        here = x * 4 + y

        def total(own, parts):
            parts = [own] + [parts[d] for d in range(15)]
            while len(parts) > 1:
                parts = [parts[i] + parts[i + 1] for i in range(0, len(parts), 2)]
            return parts[0]

        for d in range(1, 16):
            send(gpart.at[xs[d // 4] * 4 + ys[d % 4]], grecv.at[d - 1], GR_P + d, plane(d))
        for d in range(1, 16):
            got(grecv.at[d - 1], GR_P + d)
        gsum[...] = total(gpart[here], grecv)
        for d in range(1, 16):
            send(gsum, gzrecv.at[d - 1], GR_Z + d, column(d))
        for d in range(1, 16):
            got(gzrecv.at[d - 1], GR_Z + d)
        gown[here] = total(gsum[...], gzrecv)
        for d in range(1, 16):
            send(gown.at[here], gown.at[here], GR_G + d, plane(d))
        for d in range(1, 16):
            got(gown.at[xs[(4 - d // 4) % 4] * 4 + ys[(4 - d % 4) % 4]], GR_G + d)
        for d in range(1, 16):
            sent(gsum, GR_P + d)
            sent(gsum, GR_Z + d)
            sent(gsum, GR_G + d)
        drain(3)


def finish(scale, gram, skt, out_ref, work):
    lower_inverse(gram, work)
    basis_t = jnp.dot(work[...], skt[...], precision=lax.Precision.HIGHEST, preferred_element_type=F32)
    out_ref[...] = basis_t.T * scale


def local(tiles, pattern, omega):
    scale = float(256 * omega.shape[0]) ** 0.5
    vmem = pltpu.VMEM
    gram, sketch_t = pl.pallas_call(
        kernel,
        name="gauss_newton_sketch",
        out_shape=[jax.ShapeDtypeStruct((16, 8, BS), F32), jax.ShapeDtypeStruct((BS, 2 * BS), F32)],
        in_specs=[pl.BlockSpec(memory_space=pl.ANY)] * 3,
        out_specs=[pl.BlockSpec(memory_space=vmem)] * 2,
        scratch_shapes=[
            vmem((65, 4, BS, BS), BF16),
            vmem((32, BS, BS), BF16),
            vmem((4, 8, BS, BS), BF16),
            vmem((4, 8, BS, BS), BF16),
            vmem((4, 8, BS, BS), F32),
            vmem((4, 6, BS, BS), BF16),
            vmem((4, 6, BS, BS), BF16),
            vmem((4, 2, BS, BS), BF16),
            vmem((4, 2, BS, BS), F32),
            vmem((4, 2, BS, BS), BF16),
            vmem((65, BS, BS), BF16),
            vmem((PAIRS, BS, BS), F32),
            vmem((4, 6, BS, BS), BF16),
            vmem((4, 6, BS, BS), BF16),
            vmem((3, 2, BS, BS), BF16),
            vmem((3, 2, BS, BS), BF16),
            vmem((16, 8, BS), F32),
            vmem((15, 8, BS), F32),
            vmem((8, BS), F32),
            vmem((15, 8, BS), F32),
            vmem((4, 64), jnp.int32),
            vmem((8, 3 * BS), jnp.int32),
            pltpu.SMEM((8, 3 * BS), jnp.int32),
            pltpu.SemaphoreType.DMA((N_SEM,)),
            pltpu.SemaphoreType.DMA((N_SEM,)),
            pltpu.SemaphoreType.DMA((4,)),
        ],
        compiler_params=pltpu.CompilerParams(
            collective_id=0, has_side_effects=True, vmem_limit_bytes=56 * 1024 * 1024),
        cost_estimate=pl.CostEstimate(flops=2 * 2 * 256 * BS ** 3, bytes_accessed=9 * 2 ** 20, transcendentals=0),
    )(pattern.T, tiles, omega.reshape(2, BS, BS))
    return pl.pallas_call(
        functools.partial(finish, scale),
        name="cholesky_basis",
        out_shape=jax.ShapeDtypeStruct((2 * BS, BS), F32),
        in_specs=[pl.BlockSpec(memory_space=vmem)] * 2,
        out_specs=pl.BlockSpec(memory_space=vmem),
        scratch_shapes=[vmem((BS, BS), F32)],
    )(gram, sketch_t)


def solution(mesh):
    return jax.shard_map(
        local,
        mesh=mesh,
        in_specs=(P("row", "col", None, None), P("row", "col"), P(("row", "col"), None)),
        out_specs=P(("row", "col"), None),
        check_vma=False,
    )
```
